32 devices in a mesh: dp: 2 (over x), tp: 16 (over z, y, core).
Axes of the slice: x: 2, y: 2, z: 4, core: 2. Of those that a mesh axis runs over, the one named last changes fastest.
Arguments:
- queries: bfloat16 [256, 128, 576], P(('dp', 'tp')), may hold values from -10 to 10
- new_latent: bfloat16 [256, 576], P(('dp', 'tp')), may hold values from -6 to 6
- resident: bfloat16 [192, 256, 576], P(('dp', 'tp')), may hold values from -6 to 6
- leaving: bfloat16 [64, 2, 256, 576], P(('dp', 'tp')), may hold values from -6 to 6
- res_len: int32 [192], P(('dp', 'tp')), may hold values from 1 to 256, as said below
- leave_len: int32 [32, 2], replicated, may hold values from 1 to 256, as said below
- mig_dest: int32 [32, 2], replicated, may hold values from 0 to 15, as said below
- stream: bfloat16 [256, 7168], P(('dp', 'tp')), may hold values from -6 to 6
- dense_gain: float32 [7168], replicated, may hold values from 0.1 to 1.9
- w_gate: bfloat16 [7168, 18432], P('dp', 'tp'), may hold values from -0.0625 to 0.0625
- w_up: bfloat16 [7168, 18432], P('dp', 'tp'), may hold values from -0.0625 to 0.0625
- w_down: bfloat16 [18432, 7168], P('tp', 'dp'), may hold values from -0.046875 to 0.046875
- moe_gain: float32 [7168], replicated, may hold values from 0.1 to 1.9
- expert_gate: bfloat16 [16, 7168, 2048], P('tp', None, 'dp'), may hold values from -0.0625 to 0.0625
- expert_up: bfloat16 [16, 7168, 2048], P('tp', None, 'dp'), may hold values from -0.0625 to 0.0625
- expert_down: bfloat16 [16, 2048, 7168], P('tp', 'dp'), may hold values from -0.125 to 0.125
- expert_ids: int32 [256, 8], P(('dp', 'tp')), may hold values from 0 to 15, all different within a row; in each aligned block of 8 rows (0 to 7, 8 to 15, ...) at most 5 rows name the same one
- gate_scores: float32 [256, 8], P(('dp', 'tp')), may hold values from 0.05 to 1
Outputs:
- context: bfloat16 [256, 128, 512], P(('dp', 'tp'))
- arrived: bfloat16 [64, 2, 256, 576], P(('dp', 'tp'))
- stream_out: bfloat16 [256, 7168], P(('dp', 'tp'))
The draws below stay inside these ranges and needn't reach their ends.
Inputs may be any that keep to these rules, and one draw needn't show every extreme that they name: `mig_dest`: each device sends its 2 leaving requests to 2 different other devices of its dp index, and every device receives exactly 2 requests. `res_len`: some request holds all 256 positions. `leave_len`: some request holds all 256 positions. `expert_ids`: among the 8 rows of one device no expert is chosen by more than 5 rows, a bound that some block reaches; a row names 8 different experts.
All inputs are finite; a program needn't handle non-finite values.
Results may differ from the reference program's by a relative error of at most 0.023.
Values may be sent and summed in bfloat16 or wider, within the bound.
No kernel may reach another device: no remote copies, remote signals or barrier semaphores. Data moves between devices by JAX's collectives and lax.ppermute only.
A program may use at most 192 MiB of HBM per device.

```python
import math
import jax
import jax.numpy as jnp
import numpy as np
from jax import lax

D = 7168
FF = 18432
EH = 2048
HEADS = 128
VDIM = 512
QKD = 192
TOP = 8
ROWS_DEV = 8
CACHE = 256
LAYERS = 2
MIG = 2
LAT = 576
STAY = 6
EXPERTS = 16
CAP = 5
ROWS = 256
N_DP = 2
N_TP = 16
DEVICES = 32


def latent_field(key, shape):
    base_key = jax.random.fold_in(key, 0)
    values = jnp.clip(jax.random.normal(base_key, shape, jnp.float32), -6.0, 6.0)
    return values.astype(jnp.bfloat16)


def draw_queries(key, part):
    base_key = jax.random.fold_in(jax.random.fold_in(key, 11), 0)
    shape = (ROWS, HEADS, LAT)
    values = jnp.clip(jax.random.normal(base_key, shape, jnp.float32), -6.0, 6.0)
    return values.astype(jnp.bfloat16)


def draw_resident(key, part):
    return latent_field(jax.random.fold_in(key, 21), (DEVICES * STAY, CACHE, LAT))


def draw_leaving(key, part):
    return latent_field(jax.random.fold_in(key, 31), (DEVICES * MIG, LAYERS, CACHE, LAT))


def ragged_lengths(key, count, per_device):
    cap_key, len_key, pick_key = jax.random.split(key, 3)
    device_cap = jax.random.randint(cap_key, (DEVICES, 1), CACHE // 4, CACHE + 1)
    lengths = jax.random.randint(len_key, (DEVICES, per_device), 1, device_cap + 1).reshape(-1)
    pick = jax.random.randint(pick_key, (), 0, count)
    return jnp.where(jnp.arange(count) == pick, CACHE, lengths).astype(jnp.int32)


def draw_res_len(key, part):
    return ragged_lengths(jax.random.fold_in(key, 41), DEVICES * STAY, STAY)


def draw_leave_len(key, part):
    return ragged_lengths(jax.random.fold_in(key, 51), DEVICES * MIG, MIG).reshape(DEVICES, MIG)


def draw_mig_dest(key, part):
    keys = jax.random.split(jax.random.fold_in(key, 61), N_DP)
    perms = jax.vmap(lambda one: jax.random.permutation(one, N_TP))(keys).astype(jnp.int32)
    inverse = jnp.argsort(perms, axis=1, stable=True).astype(jnp.int32)
    steps = jnp.arange(MIG, dtype=jnp.int32)
    positions = (inverse[:, :, None] + 1 + steps[None, None, :]) % N_TP
    dest = jnp.take_along_axis(perms, positions.reshape(N_DP, N_TP * MIG), axis=1)
    return dest.reshape(DEVICES, MIG).astype(jnp.int32)


def block_scale(key, extent, cuts, least, top_value):
    def one(axis_at, parts):
        steps = jax.random.uniform(jax.random.fold_in(jax.random.fold_in(key, 6), axis_at), (parts,), jnp.float32, least / len(cuts), top_value / len(cuts))
        return jnp.repeat(jnp.exp(steps), extent[axis_at] // parts).reshape((-1,) + (1,) * (len(extent) - axis_at - 1))

    level = one(*cuts[0])
    for cut in cuts[1:]:
        level = level * one(*cut)
    return level


def shared_out(own_key, own, number, rows, number_of, top, most, skew):
    order = jax.random.permutation(own_key, number_of)
    packed, usual = load_shares(number_of, rows * top, most, skew, True), load_shares(number_of, rows * top, most, skew, False)
    places = jnp.arange(number_of)

    def named(tallies, rotation):
        used = int((tallies > 0).sum())
        fixed = max(1, used // 4)
        moved = fixed + (places - fixed + rotation * (used - fixed)) % max(1, number_of - fixed)
        return jnp.zeros((number_of,), jnp.int32).at[order[jnp.where(places < fixed, places, moved)]].set(jnp.asarray(tallies, jnp.int32))

    tallies = jnp.where(number % 4 == 0, named(packed, number // 4), named(usual, number - number // 4 - 1))
    mixed = jax.random.permutation(jax.random.fold_in(own, 3), number_of)
    donor, taker = mixed[0:number_of // 2 * 2:2], mixed[1:number_of // 2 * 2:2]
    slack = jnp.minimum(tallies[donor] - 1, most - tallies[taker]) // 2
    slack = jnp.where((donor == order[0]) | (taker == order[0]) | (tallies[taker] == 0), 0, jnp.maximum(slack, 0))
    moved = jax.random.randint(jax.random.fold_in(own, 4), (number_of // 2,), 0, 1 << 20) % (slack + 1)
    tallies = tallies.at[donor].add(-moved).at[taker].add(moved)
    items = jnp.searchsorted(jnp.cumsum(tallies), jnp.arange(rows * top), side="right").astype(jnp.int32)
    table = items.reshape(top, rows).T
    table = table[jax.random.permutation(jax.random.fold_in(own, 1), rows)]
    rotation = jax.random.randint(jax.random.fold_in(own, 2), (rows, 1), 0, top)
    return jnp.take_along_axis(table, (jnp.arange(top)[None, :] + rotation) % top, axis=1)


def load_shares(amount, total, bound, slope, full):
    portions = [(1 << 20) // math.isqrt(grade ** slope) + 1 for grade in range(1, amount + 1)]
    largest = bound if full else min(bound, max(-(-total // amount), total * portions[0] // sum(portions)))
    least = 1 if total - largest >= amount - 1 else 0
    given, rest = [largest] + [least] * (amount - 1), total - largest - least * (amount - 1)
    while rest > 0:
        candidates = [i for i in range(1, amount) if given[i] < largest] or [i for i in range(1, amount) if given[i] < bound]
        pool, left = sum([portions[i] for i in candidates]), rest
        for i in candidates:
            more = min(bound - given[i], max(1, left * portions[i] // pool), rest)
            given[i] = given[i] + more
            rest = rest - more
    return np.array(given)


def centred(stream_key, shape, scale, limit, shards=(), kind=jnp.bfloat16):
    entries = jax.random.normal(stream_key, shape, jnp.float32) * scale
    if len(shards) > 0:
        entries = block_scale(stream_key, shape, shards, -0.22, 0.18) * entries
    return jnp.clip(entries, min=-limit, max=limit).astype(kind)


def setup_inputs(seed: int = 0) -> dict:
    key_list = jax.random.split(jax.random.key(seed), 19)
    queries = draw_queries(jax.random.fold_in(key_list[18], 71), 0)
    new_latent = centred(key_list[1], (ROWS, LAT), 1.0, 6.0, ((0, 32),))
    resident = draw_resident(jax.random.fold_in(key_list[18], 71), 0)
    leaving = draw_leaving(jax.random.fold_in(key_list[18], 71), 0)
    res_len = draw_res_len(jax.random.fold_in(key_list[18], 71), 0)
    leave_len = draw_leave_len(jax.random.fold_in(key_list[18], 71), 0)
    mig_dest = draw_mig_dest(jax.random.fold_in(key_list[18], 71), 0)
    stream = centred(key_list[7], (ROWS, D), 1.0, 6.0, ((0, 32),))
    dense_gain = jnp.clip(1.0 + 0.18 * jax.random.normal(key_list[8], (D,), jnp.float32), 0.1, 1.9)
    w_gate = centred(key_list[9], (D, FF), D ** -0.5, 0.0625, ((0, 2), (1, 16)))
    w_up = centred(key_list[10], (D, FF), D ** -0.5, 0.0625, ((0, 2), (1, 16)))
    w_down = centred(key_list[11], (FF, D), FF ** -0.5, 0.046875, ((0, 16), (1, 2)))
    moe_gain = jnp.clip(1.0 + 0.18 * jax.random.normal(key_list[12], (D,), jnp.float32), 0.1, 1.9)
    expert_gate = centred(key_list[13], (EXPERTS, D, EH), D ** -0.5, 0.0625, ((0, 16), (2, 2)))
    expert_up = centred(key_list[14], (EXPERTS, D, EH), D ** -0.5, 0.0625, ((0, 16), (2, 2)))
    expert_down = centred(key_list[15], (EXPERTS, EH, D), EH ** -0.5, 0.125, ((0, 16), (1, 2)))
    expert_ids_keys = jax.random.split(jax.random.fold_in(key_list[16], 1), ROWS // ROWS_DEV)
    expert_ids_turns = jax.random.permutation(jax.random.fold_in(key_list[16], 3), ROWS // ROWS_DEV)
    expert_ids = jax.vmap(lambda own, number: shared_out(jax.random.fold_in(key_list[16], 2), own, number, ROWS_DEV, EXPERTS, TOP, CAP, 2))(expert_ids_keys, expert_ids_turns).reshape((ROWS, TOP))
    gate_scores = jnp.clip(jnp.exp(math.log(1.0) - 2.9957323 * jax.random.uniform(key_list[17], (ROWS, TOP), jnp.float32) ** block_scale(key_list[17], (ROWS, TOP), ((0, 32),), -0.2, 0.2)), 0.05, 1.0)
    return {"queries": queries, "new_latent": new_latent, "resident": resident, "leaving": leaving, "res_len": res_len, "leave_len": leave_len, "mig_dest": mig_dest, "stream": stream, "dense_gain": dense_gain, "w_gate": w_gate, "w_up": w_up, "w_down": w_down, "moe_gain": moe_gain, "expert_gate": expert_gate, "expert_up": expert_up, "expert_down": expert_down, "expert_ids": expert_ids, "gate_scores": gate_scores}


EPS = 1e-06
ROUTE_SCALE = 2.5

def rms_scale(rows, gain):
    values = rows.astype(jnp.float32)
    mean_square = lax.optimization_barrier(jnp.mean(values * values, axis=-1, keepdims=True))
    return (values * lax.rsqrt(mean_square + EPS) * gain).astype(jnp.bfloat16)

def attend(item):
    queries, keys, lengths, newest = item
    scale = QKD ** (-0.5)
    query_f = queries.astype(jnp.float32)
    key_f = keys.astype(jnp.float32)
    new_f = newest.astype(jnp.float32)
    scores = jnp.einsum('rhl,rcl->rhc', query_f, key_f) * scale
    positions = jnp.arange(keys.shape[1], dtype=jnp.int32)
    valid = positions[None, None, :] < lengths[:, None, None]
    masked = jnp.where(valid, scores, -1e+30)
    own_score = jnp.einsum('rhl,rl->rh', query_f, new_f) * scale
    top = jnp.maximum(lax.optimization_barrier(jnp.max(masked, axis=-1)), own_score)
    expo = jnp.where(valid, jnp.exp(masked - top[..., None]), 0.0)
    own_expo = jnp.exp(own_score - top)
    total = lax.optimization_barrier(jnp.sum(expo, axis=-1)) + own_expo
    weights = (expo / total[..., None]).astype(jnp.bfloat16)
    own_weight = (own_expo / total).astype(jnp.bfloat16)
    context = jnp.einsum('rhc,rcv->rhv', weights.astype(jnp.float32), key_f[:, :, :VDIM])
    context = context + own_weight.astype(jnp.float32)[..., None] * new_f[:, None, :VDIM]
    return context.astype(jnp.bfloat16)

def arrival_index(mig_dest):
    dest = mig_dest.reshape(N_DP, N_TP, MIG).astype(jnp.int32)
    peers = jnp.arange(N_TP, dtype=jnp.int32)
    slots = jnp.arange(MIG, dtype=jnp.int32)
    match = dest[:, None, :, :] == peers[None, :, None, None]
    is_source = jnp.any(match, axis=3)
    which = lax.optimization_barrier(jnp.sum(jnp.where(match, slots, 0), axis=3)).astype(jnp.int32)
    order = (jnp.cumsum(is_source.astype(jnp.int32), axis=2) - 1).astype(jnp.int32)
    groups = jnp.arange(N_DP, dtype=jnp.int32)[:, None]
    picks = []
    for arrival in range(MIG):
        pick = is_source & (order == arrival)
        source = lax.optimization_barrier(jnp.sum(jnp.where(pick, peers, 0), axis=2)).astype(jnp.int32)
        slot = lax.optimization_barrier(jnp.sum(jnp.where(pick, which, 0), axis=2)).astype(jnp.int32)
        picks.append((groups * N_TP + source) * MIG + slot)
    return jnp.stack(picks, axis=2).reshape(-1).astype(jnp.int32)

def run_expert(item):
    rows, gate_w, up_w, down_w = item
    block = EH // N_DP
    total = jnp.zeros((rows.shape[0], D), jnp.float32)
    for part in range(N_DP):
        gate = jnp.dot(rows, gate_w[:, part * block:(part + 1) * block], preferred_element_type=jnp.float32)
        up = jnp.dot(rows, up_w[:, part * block:(part + 1) * block], preferred_element_type=jnp.float32)
        inner = (jax.nn.silu(gate) * up).astype(jnp.bfloat16)
        piece = jnp.dot(inner, down_w[part * block:(part + 1) * block], preferred_element_type=jnp.float32)
        piece = lax.optimization_barrier(piece.astype(jnp.bfloat16))
        total = total + piece.astype(jnp.float32)
    return total.astype(jnp.bfloat16)

def reference(queries, new_latent, resident, leaving, res_len, leave_len, mig_dest, stream, dense_gain, w_gate, w_up, w_down, moe_gain, expert_gate, expert_up, expert_down, expert_ids, gate_scores):
    arrive = arrival_index(mig_dest)
    arrived = leaving[arrive]
    arrive_len = leave_len.reshape(-1)[arrive]
    keys = jnp.concatenate([resident.reshape(DEVICES, STAY, CACHE, LAT), arrived[:, 0].reshape(DEVICES, MIG, CACHE, LAT)], axis=1)
    lengths = jnp.concatenate([res_len.reshape(DEVICES, STAY), arrive_len.reshape(DEVICES, MIG)], axis=1).astype(jnp.int32)
    context = lax.map(attend, (queries.reshape(DEVICES, ROWS_DEV, HEADS, LAT), keys, lengths, new_latent.reshape(DEVICES, ROWS_DEV, LAT)))
    context = context.reshape(ROWS, HEADS, VDIM)
    normed = rms_scale(stream, dense_gain)
    gate = jnp.dot(normed, w_gate, preferred_element_type=jnp.float32)
    up = jnp.dot(normed, w_up, preferred_element_type=jnp.float32)
    hidden = (jax.nn.silu(gate) * up).astype(jnp.bfloat16)
    ffn = jnp.dot(hidden, w_down, preferred_element_type=jnp.float32)
    middle = (stream.astype(jnp.float32) + ffn).astype(jnp.bfloat16)
    mixed = rms_scale(middle, moe_gain)
    ids = expert_ids.reshape(DEVICES, ROWS_DEV, TOP).astype(jnp.int32)
    hits = (ids[..., None] == jnp.arange(EXPERTS, dtype=jnp.int32)).astype(jnp.int32)
    row_hits = lax.optimization_barrier(jnp.sum(hits, axis=2)).astype(jnp.int32)
    before = (jnp.cumsum(row_hits, axis=1) - row_hits).astype(jnp.int32)
    slot = lax.optimization_barrier(jnp.sum(hits * before[:, :, None, :], axis=3)).astype(jnp.int32)
    target = (ids * CAP + slot).astype(jnp.int32)
    device_idx = jnp.arange(DEVICES, dtype=jnp.int32)[:, None, None]
    source = jnp.broadcast_to(mixed.reshape(DEVICES, ROWS_DEV, 1, D), (DEVICES, ROWS_DEV, TOP, D))
    buffer = jnp.zeros((DEVICES, EXPERTS * CAP, D), jnp.bfloat16).at[device_idx, target].set(source)
    per_expert = buffer.reshape(DEVICES, EXPERTS, CAP, D).transpose(1, 0, 2, 3).reshape(EXPERTS, DEVICES * CAP, D)
    outputs = lax.map(run_expert, (per_expert, expert_gate, expert_up, expert_down))
    back = outputs.reshape(EXPERTS, DEVICES, CAP, D).transpose(1, 0, 2, 3).reshape(DEVICES, EXPERTS * CAP, D)
    picked = jnp.take_along_axis(back, target.reshape(DEVICES, ROWS_DEV * TOP)[:, :, None], axis=1)
    picked = picked.reshape(ROWS, TOP, D).astype(jnp.float32)
    shares = gate_scores / lax.optimization_barrier(jnp.sum(gate_scores, axis=1, keepdims=True)) * ROUTE_SCALE
    routed = jnp.einsum('rk,rkd->rd', shares, picked)
    stream_out = (middle.astype(jnp.float32) + routed).astype(jnp.bfloat16)
    return (context, arrived, stream_out)
```

```python
import jax
import jax.numpy as jnp
from jax import lax
from jax.sharding import PartitionSpec as P

VDIM = 512
QKD = 192


EPS = 1e-06
ROUTE_SCALE = 2.5
AXES = ("dp", "tp")


def rms_scale(rows, gain):
    values = rows.astype(jnp.float32)
    mean_square = jnp.mean(values * values, axis=-1, keepdims=True)
    return (values * lax.rsqrt(mean_square + EPS) * gain).astype(jnp.bfloat16)


def attend(queries, keys, lengths, newest):
    scale = QKD ** (-0.5)
    scores = jnp.einsum("rhl,rcl->rhc", queries, keys, preferred_element_type=jnp.float32) * scale
    positions = jnp.arange(keys.shape[1])
    valid = positions[None, None, :] < lengths[:, None, None]
    masked = jnp.where(valid, scores, -1e30)
    own_score = (
        jnp.einsum("rhl,rl->rh", queries, newest, preferred_element_type=jnp.float32) * scale
    )
    top = jnp.maximum(jnp.max(masked, axis=-1), own_score)
    expo = jnp.where(valid, jnp.exp(masked - top[..., None]), 0.0)
    own_expo = jnp.exp(own_score - top)
    total = jnp.sum(expo, axis=-1) + own_expo
    weights = (expo / total[..., None]).astype(jnp.bfloat16)
    own_weight = (own_expo / total).astype(jnp.bfloat16)
    context = jnp.einsum(
        "rhc,rcv->rhv", weights, keys[:, :, :VDIM], preferred_element_type=jnp.float32
    )
    context = context + own_weight.astype(jnp.float32)[..., None] * newest[:, None, :VDIM].astype(
        jnp.float32
    )
    return context.astype(jnp.bfloat16)


def swap(block, q, j):
    dp_count, tp_count = lax.axis_size("dp"), lax.axis_size("tp")
    pairs = [
        (p * tp_count + t, (p ^ q) * tp_count + (t ^ j))
        for p in range(dp_count)
        for t in range(tp_count)
    ]
    return lax.ppermute(block, AXES, pairs)


def far_masks():
    return range(4, lax.axis_size("tp"), 4)


def quad():
    return [(q, y) for q in range(lax.axis_size("dp")) for y in (0, 2) if (q, y) != (0, 0)]


def gather_far(rows):
    return jnp.stack([rows] + [swap(rows, 0, j) for j in far_masks()], axis=0)


def feature_part(rows, part, count):
    size = rows.shape[-1] // count
    return lax.dynamic_slice_in_dim(rows, part * size, size, axis=rows.ndim - 1)


def gather_parts(rows, dp_rank, dp_count):
    width = rows.shape[1]
    far = gather_far(rows).reshape(-1, width)
    parts = [feature_part(far, dp_rank, dp_count)]
    for q, y in quad():
        parts.append(swap(feature_part(far, dp_rank ^ q, dp_count), q, y))
    near = jnp.concatenate(parts, axis=0)
    return jnp.concatenate([near, swap(near, 0, 1)], axis=0)


def gather_rows(rows):
    far = gather_far(rows).reshape(-1, rows.shape[1])
    near = jnp.concatenate([far] + [swap(far, q, y) for q, y in quad()], axis=0)
    return jnp.concatenate([near, swap(near, 0, 1)], axis=0)


def realign(rows, q, dp_count):
    blocks = rows.reshape(2, dp_count, -1, rows.shape[1])
    return jnp.concatenate([blocks[:, at ^ q][:, None] for at in range(dp_count)], axis=1).reshape(rows.shape)


def wide(block):
    return block.astype(jnp.float32)


def reduce_core(total):
    half = total.shape[0] // 2
    got = swap(total[half:], 0, 1)
    return wide(total[:half]) + wide(got)


def reduce_far(total):
    out = total[0]
    for at, j in enumerate(far_masks()):
        out = out + wide(swap(total[at + 1].astype(jnp.bfloat16), 0, j))
    return out


def reduce_parts(total, dp_rank, dp_count, rows_dev):
    size = total.shape[1]
    near = reduce_core(total).reshape(dp_count, 2, -1, size)
    full = jnp.zeros((near.shape[2], size * dp_count), jnp.float32)
    for q in range(dp_count):
        if q == 0:
            part = near[0, 0]
        else:
            part = wide(swap(near[q, 0].astype(jnp.bfloat16), q, 0))
        part = part + wide(swap(near[q, 1].astype(jnp.bfloat16), q, 2))
        full = lax.dynamic_update_slice_in_dim(full, part, (dp_rank ^ q) * size, axis=1)
    return reduce_far(full.reshape(-1, rows_dev, size * dp_count))


def reduce_rows(total, dp_count, rows_dev):
    width = total.shape[1]
    near = reduce_core(total).reshape(dp_count, 2, -1, width)
    out = near[0, 0]
    for q, y in quad():
        out = out + wide(swap(near[q, y // 2].astype(jnp.bfloat16), q, y))
    return reduce_far(out.reshape(-1, rows_dev, width))


def migrate(leaving, group_dest, tp_rank):
    tp_count = lax.axis_size("tp")
    moving, layers, cache, lat = leaving.shape
    piece = layers * cache // tp_count
    outgoing = leaving.reshape(moving, tp_count, piece, lat).transpose(1, 0, 2, 3)
    spread = lax.all_to_all(outgoing, "tp", split_axis=0, concat_axis=0, tiled=True)
    packets = tp_count * moving
    dest = group_dest.reshape(-1)
    sender = jnp.arange(packets) // moving
    same = (dest[:, None] == dest[None, :]) & (sender[None, :] < sender[:, None])
    order = jnp.sum(same.astype(jnp.int32), axis=1)
    place = dest * moving + order
    source = jnp.sum(
        jnp.where(place[None, :] == jnp.arange(packets)[:, None], jnp.arange(packets)[None, :], 0),
        axis=1,
    )
    homing = jnp.take(spread.reshape(packets, piece, lat), source, axis=0)
    homing = homing.reshape(tp_count, moving, piece, lat)
    home = lax.all_to_all(homing, "tp", split_axis=0, concat_axis=0, tiled=True)
    arrived = home.transpose(1, 0, 2, 3).reshape(moving, layers, cache, lat)
    mine = lax.dynamic_slice_in_dim(source, tp_rank * moving, moving, 0)
    return arrived, mine


def on_device(
    queries,
    new_latent,
    resident,
    leaving,
    res_len,
    leave_len,
    mig_dest,
    stream,
    dense_gain,
    w_gate,
    w_up,
    w_down,
    moe_gain,
    expert_gate,
    expert_up,
    expert_down,
    expert_ids,
    gate_scores,
):
    tp_count = lax.axis_size("tp")
    dp_count = lax.axis_size("dp")
    tp_rank = lax.axis_index("tp")
    dp_rank = lax.axis_index("dp")
    group_dest = lax.dynamic_slice_in_dim(mig_dest, dp_rank * tp_count, tp_count, 0)
    group_len = lax.dynamic_slice_in_dim(leave_len, dp_rank * tp_count, tp_count, 0)
    arrived, mine = migrate(leaving, group_dest, tp_rank)
    arrived_len = jnp.take(group_len.reshape(-1), mine, axis=0)
    stay = resident.shape[0]
    context_stay = attend(queries[:stay], resident, res_len, new_latent[:stay])
    context_moved = attend(queries[stay:], arrived[:, 0], arrived_len, new_latent[stay:])
    context = jnp.concatenate([context_stay, context_moved], axis=0)

    rows_dev = stream.shape[0]
    normed = rms_scale(stream, dense_gain)
    features = gather_parts(normed, dp_rank, dp_count)
    gate_part = jnp.dot(features, w_gate, preferred_element_type=jnp.float32)
    up_part = jnp.dot(features, w_up, preferred_element_type=jnp.float32)
    gate, up = gate_part, up_part
    for q in range(1, dp_count):
        gate = gate + wide(realign(swap(gate_part.astype(jnp.bfloat16), q, 0), q, dp_count))
        up = up + wide(realign(swap(up_part.astype(jnp.bfloat16), q, 0), q, dp_count))
    hidden = (jax.nn.silu(gate) * up).astype(jnp.bfloat16)
    down = jnp.dot(hidden, w_down, preferred_element_type=jnp.float32).astype(jnp.bfloat16)
    ffn = reduce_parts(down, dp_rank, dp_count, rows_dev)
    middle = (stream.astype(jnp.float32) + ffn).astype(jnp.bfloat16)
    mixed = rms_scale(middle, moe_gain)

    shares = gate_scores / jnp.sum(gate_scores, axis=1, keepdims=True) * ROUTE_SCALE
    experts = tp_count * expert_gate.shape[0]
    chosen = expert_ids[:, :, None] == jnp.arange(experts)[None, None, :]
    table = jnp.sum(jnp.where(chosen, shares[:, :, None], 0.0), axis=1)
    high = table.astype(jnp.bfloat16)
    low = (table - wide(high)).astype(jnp.bfloat16)
    tail = jnp.pad(jnp.concatenate([high, low], axis=1), ((0, 0), (0, 128 - 2 * experts)))
    payload = jnp.concatenate([mixed, tail], axis=1)

    gathered = gather_rows(payload)
    width = mixed.shape[1]
    pooled = gathered[:, :width]
    lane = jnp.arange(128)
    mine_lane = (lane == tp_rank) | (lane == tp_rank + experts)
    row_share = jnp.sum(jnp.where(mine_lane, wide(gathered[:, width:]), 0.0), axis=1, keepdims=True)
    gate = jnp.dot(pooled, expert_gate[0], preferred_element_type=jnp.float32)
    up = jnp.dot(pooled, expert_up[0], preferred_element_type=jnp.float32)
    inner = (jax.nn.silu(gate) * up * row_share).astype(jnp.bfloat16)
    part = jnp.dot(inner, expert_down[0], preferred_element_type=jnp.float32).astype(jnp.bfloat16)
    routed = reduce_rows(part, dp_count, rows_dev)
    stream_out = (middle.astype(jnp.float32) + routed).astype(jnp.bfloat16)
    return (context, arrived, stream_out)


def solution(mesh):
    placed = (
        P(("dp", "tp"), None, None),
        P(("dp", "tp"), None),
        P(("dp", "tp"), None, None),
        P(("dp", "tp"), None, None, None),
        P(("dp", "tp")),
        P(),
        P(),
        P(("dp", "tp"), None),
        P(),
        P("dp", "tp"),
        P("dp", "tp"),
        P("tp", "dp"),
        P(),
        P("tp", None, "dp"),
        P("tp", None, "dp"),
        P("tp", "dp", None),
        P(("dp", "tp"), None),
        P(("dp", "tp"), None),
    )
    return jax.shard_map(
        on_device,
        mesh=mesh,
        in_specs=placed,
        out_specs=(
            P(("dp", "tp"), None, None),
            P(("dp", "tp"), None, None, None),
            P(("dp", "tp"), None),
        ),
        check_vma=False,
    )
```

```python
import functools

import jax
import jax.numpy as jnp
from jax import lax
from jax.experimental import pallas as pl
from jax.experimental.pallas import tpu as pltpu
from jax.sharding import PartitionSpec as P

VDIM = 512
QKD = 192


EPS = 1e-06
ROUTE_SCALE = 2.5
AXES = ("dp", "tp")
CUTS = 1
DOWN_CUTS = 2
DOWN_STEP = 896
STEP = 1024
SLOTS = 3
DENSE_STEP = 896
DENSE_VMEM = 14
HBM = pltpu.MemorySpace.HBM


def rms_scale(rows, gain):
    values = rows.astype(jnp.float32)
    mean_square = jnp.mean(values * values, axis=-1, keepdims=True)
    return (values * lax.rsqrt(mean_square + EPS) * gain).astype(jnp.bfloat16)


def attend(queries, keys, lengths, newest):
    scale = QKD ** (-0.5)
    scores = jnp.einsum("rhl,rcl->rhc", queries, keys, preferred_element_type=jnp.float32) * scale
    positions = jnp.arange(keys.shape[1])
    valid = positions[None, None, :] < lengths[:, None, None]
    masked = jnp.where(valid, scores, -1e30)
    own_score = (
        jnp.einsum("rhl,rl->rh", queries, newest, preferred_element_type=jnp.float32) * scale
    )
    top = jnp.maximum(jnp.max(masked, axis=-1), own_score)
    expo = jnp.where(valid, jnp.exp(masked - top[..., None]), 0.0)
    own_expo = jnp.exp(own_score - top)
    total = jnp.sum(expo, axis=-1) + own_expo
    weights = (expo / total[..., None]).astype(jnp.bfloat16)
    own_weight = (own_expo / total).astype(jnp.bfloat16)
    context = jnp.einsum(
        "rhc,rcv->rhv", weights, keys[:, :, :VDIM], preferred_element_type=jnp.float32
    )
    context = context + own_weight.astype(jnp.float32)[..., None] * newest[:, None, :VDIM].astype(
        jnp.float32
    )
    return context.astype(jnp.bfloat16)


def swap(block, q, j):
    dp_count, tp_count = lax.axis_size("dp"), lax.axis_size("tp")
    pairs = [
        (p * tp_count + t, (p ^ q) * tp_count + (t ^ j))
        for p in range(dp_count)
        for t in range(tp_count)
    ]
    return lax.ppermute(block, AXES, pairs)


def far_masks():
    return range(4, lax.axis_size("tp"), 4)


def quad():
    return [(q, y) for q in range(lax.axis_size("dp")) for y in (0, 2) if (q, y) != (0, 0)]


def gather_far(rows):
    return jnp.stack([rows] + [swap(rows, 0, j) for j in far_masks()], axis=0)


def feature_part(rows, part, count):
    size = rows.shape[-1] // count
    return lax.dynamic_slice_in_dim(rows, part * size, size, axis=rows.ndim - 1)


def near_parts(far, dp_rank, dp_count):
    far = far.reshape(-1, far.shape[-1])
    parts = [feature_part(far, dp_rank, dp_count)]
    for q, y in quad():
        parts.append(swap(feature_part(far, dp_rank ^ q, dp_count), q, y))
    return jnp.concatenate(parts, axis=0)


def gather_quad(far):
    far = far.reshape(-1, far.shape[-1])
    return [far] + [swap(far, q, y) for q, y in quad()]


def wide(block):
    return block.astype(jnp.float32)


def sum_dp(parts, dp_count):
    total, away = parts
    size = total.shape[0]
    for q in range(1, dp_count):
        total = total + wide(swap(away[(q - 1) * size : q * size], q, 0))
    return total


def reduce_core(mine, away, blocks):
    got = swap(away, 0, 1)
    size = mine.shape[0] // blocks
    return [wide(mine[at : at + size]) + wide(got[at : at + size]) for at in range(0, mine.shape[0], size)]


def reduce_far(blocks):
    out = blocks[0]
    for block, j in zip(blocks[1:], far_masks()):
        out = out + wide(swap(block.astype(jnp.bfloat16), 0, j))
    return out


def reduce_parts(near, dp_rank, dp_count, rows_dev):
    size = near[0].shape[1]
    parts = []
    for q in range(dp_count):
        part = near[2 * q] if q == 0 else wide(swap(near[2 * q].astype(jnp.bfloat16), q, 0))
        parts.append(part + wide(swap(near[2 * q + 1].astype(jnp.bfloat16), q, 2)))
    if dp_count == 2:
        first = dp_rank == 0
        full = jnp.concatenate([jnp.where(first, parts[0], parts[1]), jnp.where(first, parts[1], parts[0])], axis=1)
    else:
        full = jnp.zeros((parts[0].shape[0], size * dp_count), jnp.float32)
        for q in range(dp_count):
            full = lax.dynamic_update_slice_in_dim(full, parts[q], (dp_rank ^ q) * size, axis=1)
    return reduce_far([full[at : at + rows_dev] for at in range(0, full.shape[0], rows_dev)])


def reduce_rows(near, rows_dev):
    out = near[0]
    for q, y in quad():
        out = out + wide(swap(near[2 * q + y // 2].astype(jnp.bfloat16), q, y))
    return reduce_far([out[at : at + rows_dev] for at in range(0, out.shape[0], rows_dev)])


def cut_pieces(leaving):
    tp_count = lax.axis_size("tp")
    moving, layers, cache, lat = leaving.shape
    piece = layers * lat // tp_count
    turned = leaving.transpose(0, 1, 3, 2).reshape(moving, tp_count, piece, cache)
    return turned.transpose(1, 0, 2, 3)


def arrival_sources(group_dest):
    packets = group_dest.size
    moving = group_dest.shape[1]
    dest = group_dest.reshape(-1)
    at = jnp.arange(packets)
    earlier = (dest[:, None] == dest[None, :]) & (at[None, :] // moving < at[:, None] // moving)
    place = dest * moving + jnp.sum(earlier.astype(jnp.int32), axis=1)
    return jnp.sum(jnp.where(place[None, :] == at[:, None], at[None, :], 0), axis=1)


def sort_pieces(spread, source):
    packets = jnp.take(spread.reshape((-1,) + spread.shape[2:]), source, axis=0, mode="clip")
    return packets.reshape(spread.shape)


def join_pieces(home, shape):
    moving, layers, cache, lat = shape
    turned = home.transpose(1, 0, 2, 3).reshape(moving, layers, lat, cache)
    return turned.transpose(0, 1, 3, 2)


def in_hbm(weights):
    return pltpu.with_memory_space_constraint(weights, HBM)


def ring(copies, slots):
    count, make = copies
    for at in range(min(slots, count)):
        make(at).start()

    def free(at):
        @pl.when(at + slots < count)
        def _():
            make(at + slots).start()

    return (lambda at: make(at).wait()), free


def dense_kernel(groups, near_ref, other_ref, hbm, own_ref, away_ref, rows_ref, buf, sem):
    size = near_ref.shape[0] // groups
    steps = near_ref.shape[1] // DENSE_STEP

    def make(at):
        slot = lax.rem(at, SLOTS)
        return pltpu.make_async_copy(
            hbm.at[pl.ds(at * DENSE_STEP, DENSE_STEP)], buf.at[slot], sem.at[slot]
        )

    wait, free = ring((steps, make), SLOTS)
    for at in range(groups):
        part = slice(at * size, (at + 1) * size)
        rows_ref[2 * at * size : (2 * at + 1) * size] = near_ref[part]
        rows_ref[(2 * at + 1) * size : (2 * at + 2) * size] = other_ref[part]
    acc = jnp.zeros((rows_ref.shape[0], own_ref.shape[1]), jnp.float32)
    for at in range(steps):
        wait(at)
        rows = rows_ref[:, at * DENSE_STEP : (at + 1) * DENSE_STEP]
        acc = acc + jnp.dot(rows, buf[at % SLOTS], preferred_element_type=jnp.float32)
        free(at)
    own = own_ref.shape[0]
    own_ref[...] = acc[:own]
    away_ref[...] = acc[own:].astype(jnp.bfloat16)


def run_dense(near, other, weights, groups):
    count, width = 2 * near.shape[0], weights.shape[1]
    vmem, far = pl.BlockSpec(memory_space=pltpu.VMEM), pl.BlockSpec(memory_space=HBM)
    own = count // groups
    return pl.pallas_call(
        functools.partial(dense_kernel, groups),
        out_shape=(
            jax.ShapeDtypeStruct((own, width), jnp.float32),
            jax.ShapeDtypeStruct((count - own, width), jnp.bfloat16),
        ),
        in_specs=[vmem, vmem, far],
        out_specs=(vmem, vmem),
        scratch_shapes=[
            pltpu.VMEM((count, near.shape[1]), jnp.bfloat16),
            pltpu.VMEM((SLOTS, DENSE_STEP, width), jnp.bfloat16),
            pltpu.SemaphoreType.DMA((SLOTS,)),
        ],
        compiler_params=pltpu.CompilerParams(vmem_limit_bytes=DENSE_VMEM * 1024 * 1024),
    )(near, other, in_hbm(weights))


def up_kernel(first, last, base, width, experts, *refs):
    refs = list(refs)
    near_ref, other_ref, gate_hbm, up_hbm = refs[:4]
    del refs[:4]
    if not first:
        gate_in, up_in, share_in = refs[:3]
        del refs[:3]
    if last:
        inner_ref = refs.pop(0)
        gate_acc, up_acc = refs.pop(0), refs.pop(0)
    else:
        gate_acc, up_acc, share_out = refs[:3]
        del refs[:3]
    gate_buf, up_buf, gate_sem, up_sem = refs
    count = width // STEP

    def copies(hbm, buf, sem):
        def make(at):
            slot = lax.rem(at, SLOTS)
            return pltpu.make_async_copy(
                hbm.at[0, pl.ds(base + at * STEP, STEP)], buf.at[slot], sem.at[slot]
            )

        return count, make

    gate_wait, gate_free = ring(copies(gate_hbm, gate_buf, gate_sem), SLOTS)
    up_wait, up_free = ring(copies(up_hbm, up_buf, up_sem), SLOTS)
    if first:
        gate_acc[...] = jnp.zeros_like(gate_acc)
        up_acc[...] = jnp.zeros_like(up_acc)
        lane = lax.broadcasted_iota(jnp.int32, (1, 128), 1)
        rank = lax.axis_index("tp")
        mine = (lane == rank) | (lane == rank + experts)
        tail = jnp.concatenate([near_ref[:, width:], other_ref[:, width:]], axis=0)
        tail = jnp.where(mine, tail.astype(jnp.float32), 0.0)
        share = jnp.sum(tail, axis=1, keepdims=True)
    else:
        gate_acc[...] = gate_in[...]
        up_acc[...] = up_in[...]
        share = share_in[:, :1]
    if not last:
        share_out[...] = jnp.broadcast_to(share, share_out.shape)

    @pl.loop(0, count)
    def _(at):
        where = pl.ds(pl.multiple_of(at * STEP, 128), STEP)
        rows = jnp.concatenate([near_ref[:, where], other_ref[:, where]], axis=0)
        slot = lax.rem(at, SLOTS)
        gate_wait(at)
        gate_acc[...] += jnp.dot(rows, gate_buf[slot], preferred_element_type=jnp.float32)
        gate_free(at)
        up_wait(at)
        up_acc[...] += jnp.dot(rows, up_buf[slot], preferred_element_type=jnp.float32)
        up_free(at)

    if last:
        gate = gate_acc[...]
        inner_ref[...] = (gate / (1.0 + jnp.exp(-gate)) * up_acc[...] * share).astype(jnp.bfloat16)


def run_up(cut, near, other, gate_w, up_w, state, width, experts):
    first, last = cut == 0, cut == CUTS - 1
    count, hidden = 2 * near.shape[0], gate_w.shape[2]
    vmem, far = pl.BlockSpec(memory_space=pltpu.VMEM), pl.BlockSpec(memory_space=HBM)
    total = jax.ShapeDtypeStruct((count, hidden), jnp.float32)
    inner = jax.ShapeDtypeStruct((count, hidden), jnp.bfloat16)
    share = jax.ShapeDtypeStruct((count, 128), jnp.float32)
    scratch = [pltpu.VMEM((count, hidden), jnp.float32)] * 2 if last else []
    return pl.pallas_call(
        functools.partial(up_kernel, first, last, cut * width, width, experts),
        out_shape=inner if last else (total, total, share),
        in_specs=[vmem, vmem, far, far] + [vmem] * len(state),
        out_specs=vmem if last else (vmem, vmem, vmem),
        scratch_shapes=scratch
        + [pltpu.VMEM((SLOTS, STEP, hidden), jnp.bfloat16)] * 2
        + [pltpu.SemaphoreType.DMA((SLOTS,))] * 2,
        compiler_params=pltpu.CompilerParams(vmem_limit_bytes=18 * 1024 * 1024),
    )(near, other, in_hbm(gate_w), in_hbm(up_w), *state)


def down_kernel(base, inner_ref, down_hbm, near_ref, away_ref, buf, sem):
    half, width = near_ref.shape

    def make(at):
        slot = lax.rem(at, SLOTS)
        where = pl.ds(base + at * DOWN_STEP, DOWN_STEP)
        return pltpu.make_async_copy(down_hbm.at[0, :, where], buf.at[slot], sem.at[slot])

    wait, free = ring((width // DOWN_STEP, make), SLOTS)

    @pl.loop(0, width // DOWN_STEP)
    def _(at):
        wait(at)
        where = pl.ds(pl.multiple_of(at * DOWN_STEP, 128), DOWN_STEP)
        out = jnp.dot(inner_ref[...], buf[lax.rem(at, SLOTS)], preferred_element_type=jnp.float32)
        near_ref[:, where] = out[:half].astype(jnp.bfloat16)
        away_ref[:, where] = out[half:].astype(jnp.bfloat16)
        free(at)


def run_down(cut, inner, down_w, width):
    count, hidden = inner.shape
    vmem, far = pl.BlockSpec(memory_space=pltpu.VMEM), pl.BlockSpec(memory_space=HBM)
    half = jax.ShapeDtypeStruct((count // 2, width), jnp.bfloat16)
    return pl.pallas_call(
        functools.partial(down_kernel, cut * width),
        out_shape=(half, half),
        in_specs=[vmem, far],
        out_specs=(vmem, vmem),
        scratch_shapes=[
            pltpu.VMEM((SLOTS, hidden, DOWN_STEP), jnp.bfloat16),
            pltpu.SemaphoreType.DMA((SLOTS,)),
        ],
        compiler_params=pltpu.CompilerParams(vmem_limit_bytes=12 * 1024 * 1024),
    )(inner, in_hbm(down_w))


def on_device(
    queries,
    new_latent,
    resident,
    leaving,
    res_len,
    leave_len,
    mig_dest,
    stream,
    dense_gain,
    w_gate,
    w_up,
    w_down,
    moe_gain,
    expert_gate,
    expert_up,
    expert_down,
    expert_ids,
    gate_scores,
):
    tp_count = lax.axis_size("tp")
    dp_count = lax.axis_size("dp")
    tp_rank = lax.axis_index("tp")
    dp_rank = lax.axis_index("dp")
    group_dest = lax.dynamic_slice_in_dim(mig_dest, dp_rank * tp_count, tp_count, 0)
    group_len = lax.dynamic_slice_in_dim(leave_len, dp_rank * tp_count, tp_count, 0)
    rows_dev = stream.shape[0]
    normed = rms_scale(stream, dense_gain)
    near = near_parts(gather_far(normed), dp_rank, dp_count)
    other = swap(near, 0, 1)
    near, outgoing = lax.optimization_barrier((near, cut_pieces(leaving)))
    spread = lax.all_to_all(outgoing, "tp", split_axis=0, concat_axis=0, tiled=True)
    gate = sum_dp(run_dense(near, other, w_gate, dp_count), dp_count)
    up = sum_dp(run_dense(near, other, w_up, dp_count), dp_count)
    hidden = (jax.nn.silu(gate) * up).astype(jnp.bfloat16)
    near = []
    for q in range(dp_count):
        block = swap(hidden, q, 0) if q else hidden
        down = jnp.dot(block, w_down, preferred_element_type=jnp.float32).astype(jnp.bfloat16)
        half = down.shape[0] // 2
        near += reduce_core(down[:half], down[half:], 2)
    near[-1], spread = lax.optimization_barrier((near[-1], spread))
    ffn = reduce_parts(near, dp_rank, dp_count, rows_dev)
    middle = (stream.astype(jnp.float32) + ffn).astype(jnp.bfloat16)
    mixed = rms_scale(middle, moe_gain)

    shares = gate_scores / jnp.sum(gate_scores, axis=1, keepdims=True) * ROUTE_SCALE
    experts = tp_count * expert_gate.shape[0]
    chosen = expert_ids[:, :, None] == jnp.arange(experts)[None, None, :]
    table = jnp.sum(jnp.where(chosen, shares[:, :, None], 0.0), axis=1)
    high = table.astype(jnp.bfloat16)
    low = (table - wide(high)).astype(jnp.bfloat16)
    tail = jnp.pad(jnp.concatenate([high, low], axis=1), ((0, 0), (0, 128 - 2 * experts)))
    width = mixed.shape[1] // CUTS
    pieces = [mixed[:, at * width : (at + 1) * width] for at in range(CUTS)]
    pieces[0] = jnp.concatenate([pieces[0], tail], axis=1)
    homing = sort_pieces(spread, arrival_sources(group_dest))
    near = []
    for piece in pieces:
        blocks = gather_quad(gather_far(piece))
        blocks[1], homing = lax.optimization_barrier((blocks[1], homing))
        near.append(jnp.concatenate(blocks, axis=0))
    state = ()
    for at in range(CUTS):
        state = run_up(at, near[at], swap(near[at], 0, 1), expert_gate, expert_up, state, width, experts)
    out = []
    width = mixed.shape[1] // DOWN_CUTS
    sums = [reduce_core(*run_down(at, state, expert_down, width), 2 * dp_count) for at in range(DOWN_CUTS)]
    home = lax.all_to_all(homing, "tp", split_axis=0, concat_axis=0, tiled=True)
    sums[-1][0], home = lax.optimization_barrier((sums[-1][0], home))
    arrived = join_pieces(home, leaving.shape)
    for at in range(DOWN_CUTS):
        routed = reduce_rows(sums[at], rows_dev)
        out.append(wide(middle[:, at * width : (at + 1) * width]) + routed)
    moving = leaving.shape[0]
    source = arrival_sources(group_dest)
    mine = lax.dynamic_slice_in_dim(source, tp_rank * moving, moving, 0)
    arrived_len = jnp.take(group_len.reshape(-1), mine, axis=0, mode="clip")
    stay = resident.shape[0]
    context_stay = attend(queries[:stay], resident, res_len, new_latent[:stay])
    context_moved = attend(queries[stay:], arrived[:, 0], arrived_len, new_latent[stay:])
    context = jnp.concatenate([context_stay, context_moved], axis=0)

    stream_out = jnp.concatenate(out, axis=1).astype(jnp.bfloat16)
    return (context, arrived, stream_out)


def solution(mesh):
    placed = (
        P(("dp", "tp"), None, None),
        P(("dp", "tp"), None),
        P(("dp", "tp"), None, None),
        P(("dp", "tp"), None, None, None),
        P(("dp", "tp")),
        P(),
        P(),
        P(("dp", "tp"), None),
        P(),
        P("dp", "tp"),
        P("dp", "tp"),
        P("tp", "dp"),
        P(),
        P("tp", None, "dp"),
        P("tp", None, "dp"),
        P("tp", "dp", None),
        P(("dp", "tp"), None),
        P(("dp", "tp"), None),
    )
    return jax.shard_map(
        on_device,
        mesh=mesh,
        in_specs=placed,
        out_specs=(
            P(("dp", "tp"), None, None),
            P(("dp", "tp"), None, None, None),
            P(("dp", "tp"), None),
        ),
        check_vma=False,
    )
```

```python
import functools

import jax
import jax.numpy as jnp
from jax import lax
from jax.experimental import pallas as pl
from jax.experimental.pallas import tpu as pltpu
from jax.sharding import PartitionSpec as P

VDIM = 512
QKD = 192


EPS = 1e-06
ROUTE_SCALE = 2.5
AXES = ("dp", "tp")
CUTS = 2
DOWN_CUTS = 2
DOWN_STEP = 896
STEP = 1024
SLOTS = 3
DENSE_STEP = 896
DENSE_VMEM = 14
HBM = pltpu.MemorySpace.HBM


def rms_scale(rows, gain):
    values = rows.astype(jnp.float32)
    mean_square = jnp.mean(values * values, axis=-1, keepdims=True)
    return (values * lax.rsqrt(mean_square + EPS) * gain).astype(jnp.bfloat16)


def attend(queries, keys, lengths, newest):
    scale = QKD ** (-0.5)
    scores = jnp.einsum("rhl,rcl->rhc", queries, keys, preferred_element_type=jnp.float32) * scale
    positions = jnp.arange(keys.shape[1])
    valid = positions[None, None, :] < lengths[:, None, None]
    masked = jnp.where(valid, scores, -1e30)
    own_score = (
        jnp.einsum("rhl,rl->rh", queries, newest, preferred_element_type=jnp.float32) * scale
    )
    top = jnp.maximum(jnp.max(masked, axis=-1), own_score)
    expo = jnp.where(valid, jnp.exp(masked - top[..., None]), 0.0)
    own_expo = jnp.exp(own_score - top)
    total = jnp.sum(expo, axis=-1) + own_expo
    weights = (expo / total[..., None]).astype(jnp.bfloat16)
    own_weight = (own_expo / total).astype(jnp.bfloat16)
    context = jnp.einsum(
        "rhc,rcv->rhv", weights, keys[:, :, :VDIM], preferred_element_type=jnp.float32
    )
    context = context + own_weight.astype(jnp.float32)[..., None] * newest[:, None, :VDIM].astype(
        jnp.float32
    )
    return context.astype(jnp.bfloat16)


def swap(block, q, j):
    dp_count, tp_count = lax.axis_size("dp"), lax.axis_size("tp")
    pairs = [
        (p * tp_count + t, (p ^ q) * tp_count + (t ^ j))
        for p in range(dp_count)
        for t in range(tp_count)
    ]
    return lax.ppermute(block, AXES, pairs)


def far_masks():
    return range(4, lax.axis_size("tp"), 4)


def quad():
    return [(q, y) for q in range(lax.axis_size("dp")) for y in (0, 2) if (q, y) != (0, 0)]


def gather_far(rows):
    return jnp.stack([rows] + [swap(rows, 0, j) for j in far_masks()], axis=0)


def feature_part(rows, part, count):
    size = rows.shape[-1] // count
    return lax.dynamic_slice_in_dim(rows, part * size, size, axis=rows.ndim - 1)


def near_parts(far, dp_rank, dp_count):
    far = far.reshape(-1, far.shape[-1])
    parts = [feature_part(far, dp_rank, dp_count)]
    for q, y in quad():
        parts.append(swap(feature_part(far, dp_rank ^ q, dp_count), q, y))
    return jnp.concatenate(parts, axis=0)


def gather_quad(far):
    far = far.reshape(-1, far.shape[-1])
    return [far] + [swap(far, q, y) for q, y in quad()]


def wide(block):
    return block.astype(jnp.float32)


def sum_dp(parts, dp_count):
    total, away = parts
    size = total.shape[0]
    for q in range(1, dp_count):
        total = total + wide(swap(away[(q - 1) * size : q * size], q, 0))
    return total


def reduce_core(mine, away, blocks):
    got = swap(away, 0, 1)
    size = mine.shape[0] // blocks
    return [wide(mine[at : at + size]) + wide(got[at : at + size]) for at in range(0, mine.shape[0], size)]


def reduce_far(blocks):
    out = blocks[0]
    for block, j in zip(blocks[1:], far_masks()):
        out = out + wide(swap(block.astype(jnp.bfloat16), 0, j))
    return out


def reduce_parts(near, dp_rank, dp_count, rows_dev):
    size = near[0].shape[1]
    parts = []
    for q in range(dp_count):
        part = near[2 * q] if q == 0 else wide(swap(near[2 * q].astype(jnp.bfloat16), q, 0))
        parts.append(part + wide(swap(near[2 * q + 1].astype(jnp.bfloat16), q, 2)))
    if dp_count == 2:
        first = dp_rank == 0
        full = jnp.concatenate([jnp.where(first, parts[0], parts[1]), jnp.where(first, parts[1], parts[0])], axis=1)
    else:
        full = jnp.zeros((parts[0].shape[0], size * dp_count), jnp.float32)
        for q in range(dp_count):
            full = lax.dynamic_update_slice_in_dim(full, parts[q], (dp_rank ^ q) * size, axis=1)
    return reduce_far([full[at : at + rows_dev] for at in range(0, full.shape[0], rows_dev)])


def reduce_rows(near, rows_dev):
    out = near[0]
    for q, y in quad():
        out = out + wide(swap(near[2 * q + y // 2].astype(jnp.bfloat16), q, y))
    return reduce_far([out[at : at + rows_dev] for at in range(0, out.shape[0], rows_dev)])


def cut_pieces(leaving):
    tp_count = lax.axis_size("tp")
    moving, layers, cache, lat = leaving.shape
    piece = layers * lat // tp_count
    turned = leaving.transpose(0, 1, 3, 2).reshape(moving, tp_count, piece, cache)
    return turned.transpose(1, 0, 2, 3)


def arrival_sources(group_dest):
    packets = group_dest.size
    moving = group_dest.shape[1]
    dest = group_dest.reshape(-1)
    at = jnp.arange(packets)
    earlier = (dest[:, None] == dest[None, :]) & (at[None, :] // moving < at[:, None] // moving)
    place = dest * moving + jnp.sum(earlier.astype(jnp.int32), axis=1)
    return jnp.sum(jnp.where(place[None, :] == at[:, None], at[None, :], 0), axis=1)


def sort_pieces(spread, source):
    packets = jnp.take(spread.reshape((-1,) + spread.shape[2:]), source, axis=0, mode="clip")
    return packets.reshape(spread.shape)


def join_pieces(home, shape):
    moving, layers, cache, lat = shape
    turned = home.transpose(1, 0, 2, 3).reshape(moving, layers, lat, cache)
    return turned.transpose(0, 1, 3, 2)


def in_hbm(weights):
    return pltpu.with_memory_space_constraint(weights, HBM)


def ring(copies, slots):
    count, make = copies
    for at in range(min(slots, count)):
        make(at).start()

    def free(at):
        @pl.when(at + slots < count)
        def _():
            make(at + slots).start()

    return (lambda at: make(at).wait()), free


def dense_kernel(groups, near_ref, other_ref, hbm, own_ref, away_ref, rows_ref, buf, sem):
    size = near_ref.shape[0] // groups
    steps = near_ref.shape[1] // DENSE_STEP

    def make(at):
        slot = lax.rem(at, SLOTS)
        return pltpu.make_async_copy(
            hbm.at[pl.ds(at * DENSE_STEP, DENSE_STEP)], buf.at[slot], sem.at[slot]
        )

    wait, free = ring((steps, make), SLOTS)
    for at in range(groups):
        part = slice(at * size, (at + 1) * size)
        rows_ref[2 * at * size : (2 * at + 1) * size] = near_ref[part]
        rows_ref[(2 * at + 1) * size : (2 * at + 2) * size] = other_ref[part]
    acc = jnp.zeros((rows_ref.shape[0], own_ref.shape[1]), jnp.float32)
    for at in range(steps):
        wait(at)
        rows = rows_ref[:, at * DENSE_STEP : (at + 1) * DENSE_STEP]
        acc = acc + jnp.dot(rows, buf[at % SLOTS], preferred_element_type=jnp.float32)
        free(at)
    own = own_ref.shape[0]
    own_ref[...] = acc[:own]
    away_ref[...] = acc[own:].astype(jnp.bfloat16)


def run_dense(near, other, weights, groups):
    count, width = 2 * near.shape[0], weights.shape[1]
    vmem, far = pl.BlockSpec(memory_space=pltpu.VMEM), pl.BlockSpec(memory_space=HBM)
    own = count // groups
    return pl.pallas_call(
        functools.partial(dense_kernel, groups),
        out_shape=(
            jax.ShapeDtypeStruct((own, width), jnp.float32),
            jax.ShapeDtypeStruct((count - own, width), jnp.bfloat16),
        ),
        in_specs=[vmem, vmem, far],
        out_specs=(vmem, vmem),
        scratch_shapes=[
            pltpu.VMEM((count, near.shape[1]), jnp.bfloat16),
            pltpu.VMEM((SLOTS, DENSE_STEP, width), jnp.bfloat16),
            pltpu.SemaphoreType.DMA((SLOTS,)),
        ],
        compiler_params=pltpu.CompilerParams(vmem_limit_bytes=DENSE_VMEM * 1024 * 1024),
    )(near, other, in_hbm(weights))


def expert_kernel(outs, experts, *refs):
    parts, refs = refs[:2], refs[2:]
    gate_hbm, up_hbm, down_hbm = refs[:3]
    results, refs = refs[3 : 3 + 2 * outs], refs[3 + 2 * outs :]
    rows_ref, tail_ref, inner_ref, gate_buf, up_buf, down_buf, gate_acc, up_acc, row_sem, gate_sem, up_sem, down_sem = refs
    half, width = rows_ref.shape[0] // 2, rows_ref.shape[1]
    span = width // outs

    def copies(hbm, buf, sem):
        def make(at):
            slot = lax.rem(at, SLOTS)
            return pltpu.make_async_copy(
                hbm.at[0, pl.ds(at * STEP, STEP)], buf.at[slot], sem.at[slot]
            )

        return width // STEP, make

    def make_down(at):
        slot = lax.rem(at, SLOTS)
        where = pl.ds(pl.multiple_of(at * DOWN_STEP, 128), DOWN_STEP)
        return pltpu.make_async_copy(down_hbm.at[0, :, where], down_buf.at[slot], down_sem.at[slot])

    moves = []
    for side in range(2):
        where = pl.ds(side * half, half)
        moves.append((parts[side].at[:, pl.ds(0, width)], rows_ref.at[where]))
        moves.append((parts[side].at[:, pl.ds(width, 128)], tail_ref.at[where]))
    moves = [pltpu.make_async_copy(*move, row_sem.at[at]) for at, move in enumerate(moves)]
    for move in moves:
        move.start()
    gate_wait, gate_free = ring(copies(gate_hbm, gate_buf, gate_sem), SLOTS)
    up_wait, up_free = ring(copies(up_hbm, up_buf, up_sem), SLOTS)
    down_wait, down_free = ring((width // DOWN_STEP, make_down), SLOTS)
    gate_acc[...] = jnp.zeros_like(gate_acc)
    up_acc[...] = jnp.zeros_like(up_acc)
    for move in moves:
        move.wait()

    @pl.loop(0, width // STEP)
    def _(at):
        rows = rows_ref[:, pl.ds(pl.multiple_of(at * STEP, 128), STEP)]
        slot = lax.rem(at, SLOTS)
        gate_wait(at)
        gate_acc[...] += jnp.dot(rows, gate_buf[slot], preferred_element_type=jnp.float32)
        gate_free(at)
        up_wait(at)
        up_acc[...] += jnp.dot(rows, up_buf[slot], preferred_element_type=jnp.float32)
        up_free(at)

    lane = lax.broadcasted_iota(jnp.int32, (1, 128), 1)
    rank = lax.axis_index("tp")
    mine = (lane == rank) | (lane == rank + experts)
    share = jnp.sum(jnp.where(mine, tail_ref[...].astype(jnp.float32), 0.0), axis=1, keepdims=True)
    gate = gate_acc[...]
    inner_ref[...] = (gate / (1.0 + jnp.exp(-gate)) * up_acc[...] * share).astype(jnp.bfloat16)

    for one in range(outs):
        near_ref, away_ref = results[2 * one : 2 * one + 2]
        first = one * (span // DOWN_STEP)

        @pl.loop(0, span // DOWN_STEP)
        def _(step, near_ref=near_ref, away_ref=away_ref, first=first):
            at = first + step
            down_wait(at)
            where = pl.ds(pl.multiple_of(step * DOWN_STEP, 128), DOWN_STEP)
            weights = down_buf[lax.rem(at, SLOTS)]
            out = jnp.dot(inner_ref[...], weights, preferred_element_type=jnp.float32)
            near_ref[:, where] = out[:half].astype(jnp.bfloat16)
            away_ref[:, where] = out[half:].astype(jnp.bfloat16)
            down_free(at)


def run_expert(near, other, gate_w, up_w, down_w, experts):
    count, width, hidden = 2 * near.shape[0], gate_w.shape[1], gate_w.shape[2]
    vmem, far = pl.BlockSpec(memory_space=pltpu.VMEM), pl.BlockSpec(memory_space=HBM)
    total = pltpu.VMEM((count, hidden), jnp.float32)
    weights = pltpu.VMEM((SLOTS, STEP, hidden), jnp.bfloat16)
    half = jax.ShapeDtypeStruct((count // 2, width // DOWN_CUTS), jnp.bfloat16)
    sems = pltpu.SemaphoreType.DMA((SLOTS,))
    out = pl.pallas_call(
        functools.partial(expert_kernel, DOWN_CUTS, experts),
        out_shape=(half,) * (2 * DOWN_CUTS),
        in_specs=[pl.BlockSpec(memory_space=pl.ANY)] * 2 + [far] * 3,
        out_specs=(vmem,) * (2 * DOWN_CUTS),
        scratch_shapes=[
            pltpu.VMEM((count, width), jnp.bfloat16),
            pltpu.VMEM((count, 128), jnp.bfloat16),
            pltpu.VMEM((count, hidden), jnp.bfloat16),
            weights,
            weights,
            pltpu.VMEM((SLOTS, hidden, DOWN_STEP), jnp.bfloat16),
            total,
            total,
            pltpu.SemaphoreType.DMA((4,)),
            sems,
            sems,
            sems,
        ],
        compiler_params=pltpu.CompilerParams(vmem_limit_bytes=32 * 1024 * 1024),
    )(near, other, in_hbm(gate_w), in_hbm(up_w), in_hbm(down_w))
    return [out[2 * at : 2 * at + 2] for at in range(DOWN_CUTS)]


def on_device(
    queries,
    new_latent,
    resident,
    leaving,
    res_len,
    leave_len,
    mig_dest,
    stream,
    dense_gain,
    w_gate,
    w_up,
    w_down,
    moe_gain,
    expert_gate,
    expert_up,
    expert_down,
    expert_ids,
    gate_scores,
):
    tp_count = lax.axis_size("tp")
    dp_count = lax.axis_size("dp")
    tp_rank = lax.axis_index("tp")
    dp_rank = lax.axis_index("dp")
    group_dest = lax.dynamic_slice_in_dim(mig_dest, dp_rank * tp_count, tp_count, 0)
    group_len = lax.dynamic_slice_in_dim(leave_len, dp_rank * tp_count, tp_count, 0)
    rows_dev = stream.shape[0]
    normed = rms_scale(stream, dense_gain)
    near = near_parts(gather_far(normed), dp_rank, dp_count)
    other = swap(near, 0, 1)
    near, outgoing = lax.optimization_barrier((near, cut_pieces(leaving)))
    gate_parts = run_dense(near, other, w_gate, dp_count)
    spread = lax.all_to_all(outgoing, "tp", split_axis=0, concat_axis=0, tiled=True)
    gate = sum_dp(gate_parts, dp_count)
    up = sum_dp(run_dense(near, other, w_up, dp_count), dp_count)
    hidden = (jax.nn.silu(gate) * up).astype(jnp.bfloat16)
    near = []
    for q in range(dp_count):
        block = swap(hidden, q, 0) if q else hidden
        down = jnp.dot(block, w_down, preferred_element_type=jnp.float32).astype(jnp.bfloat16)
        half = down.shape[0] // 2
        near += reduce_core(down[:half], down[half:], 2)
    stay = resident.shape[0]
    context_stay = attend(queries[:stay], resident, res_len, new_latent[:stay])
    near[-1], context_stay = lax.optimization_barrier((near[-1], context_stay))
    near[0], spread = lax.optimization_barrier((near[0], spread))
    ffn = reduce_parts(near, dp_rank, dp_count, rows_dev)
    middle = (stream.astype(jnp.float32) + ffn).astype(jnp.bfloat16)
    mixed = rms_scale(middle, moe_gain)

    shares = gate_scores / jnp.sum(gate_scores, axis=1, keepdims=True) * ROUTE_SCALE
    experts = tp_count * expert_gate.shape[0]
    chosen = expert_ids[:, :, None] == jnp.arange(experts)[None, None, :]
    table = jnp.sum(jnp.where(chosen, shares[:, :, None], 0.0), axis=1)
    high = table.astype(jnp.bfloat16)
    low = (table - wide(high)).astype(jnp.bfloat16)
    tail = jnp.pad(jnp.concatenate([high, low], axis=1), ((0, 0), (0, 128 - 2 * experts)))
    width = mixed.shape[1] // CUTS
    pieces = [mixed[:, at * width : (at + 1) * width] for at in range(CUTS)]
    pieces[-1] = jnp.concatenate([pieces[-1], tail], axis=1)
    homing = sort_pieces(spread, arrival_sources(group_dest))
    cuts = [gather_quad(gather_far(piece)) for piece in pieces]
    cuts[0][-1], homing = lax.optimization_barrier((cuts[0][-1], homing))
    near = jnp.concatenate([jnp.concatenate(row, axis=1) for row in zip(*cuts)], axis=0)
    halves = run_expert(near, swap(near, 0, 1), expert_gate, expert_up, expert_down, experts)
    out = []
    width = mixed.shape[1] // DOWN_CUTS
    sums = [reduce_core(*half, 2 * dp_count) for half in halves]
    home = lax.all_to_all(homing, "tp", split_axis=0, concat_axis=0, tiled=True)
    arrived = join_pieces(home, leaving.shape)
    for at in range(DOWN_CUTS):
        routed = reduce_rows(sums[at], rows_dev)
        out.append(wide(middle[:, at * width : (at + 1) * width]) + routed)
    moving = leaving.shape[0]
    source = arrival_sources(group_dest)
    mine = lax.dynamic_slice_in_dim(source, tp_rank * moving, moving, 0)
    arrived_len = jnp.take(group_len.reshape(-1), mine, axis=0, mode="clip")
    context_moved = attend(queries[stay:], arrived[:, 0], arrived_len, new_latent[stay:])
    context = jnp.concatenate([context_stay, context_moved], axis=0)

    stream_out = jnp.concatenate(out, axis=1).astype(jnp.bfloat16)
    return (context, arrived, stream_out)


def solution(mesh):
    placed = (
        P(("dp", "tp"), None, None),
        P(("dp", "tp"), None),
        P(("dp", "tp"), None, None),
        P(("dp", "tp"), None, None, None),
        P(("dp", "tp")),
        P(),
        P(),
        P(("dp", "tp"), None),
        P(),
        P("dp", "tp"),
        P("dp", "tp"),
        P("tp", "dp"),
        P(),
        P("tp", None, "dp"),
        P("tp", None, "dp"),
        P("tp", "dp", None),
        P(("dp", "tp"), None),
        P(("dp", "tp"), None),
    )
    return jax.shard_map(
        on_device,
        mesh=mesh,
        in_specs=placed,
        out_specs=(
            P(("dp", "tp"), None, None),
            P(("dp", "tp"), None, None, None),
            P(("dp", "tp"), None),
        ),
        check_vma=False,
    )
```

```python
import functools

import jax
import jax.numpy as jnp
from jax import lax
from jax.experimental import pallas as pl
from jax.experimental.pallas import tpu as pltpu
from jax.sharding import PartitionSpec as P

VDIM = 512
QKD = 192


EPS = 1e-06
ROUTE_SCALE = 2.5
AXES = ("dp", "tp")
CUTS = 2
DOWN_CUTS = 2
DOWN_STEP = 896
STEP = 1024
SLOTS = 3
DENSE_STEP = 896
DENSE_VMEM = 14
HBM = pltpu.MemorySpace.HBM


def rms_scale(rows, gain):
    values = rows.astype(jnp.float32)
    mean_square = jnp.mean(values * values, axis=-1, keepdims=True)
    return (values * lax.rsqrt(mean_square + EPS) * gain).astype(jnp.bfloat16)


def attend(queries, keys, lengths, newest):
    scale = QKD ** (-0.5)
    scores = jnp.einsum("rhl,rcl->rhc", queries, keys, preferred_element_type=jnp.float32) * scale
    positions = jnp.arange(keys.shape[1])
    valid = positions[None, None, :] < lengths[:, None, None]
    masked = jnp.where(valid, scores, -1e30)
    own_score = (
        jnp.einsum("rhl,rl->rh", queries, newest, preferred_element_type=jnp.float32) * scale
    )
    top = jnp.maximum(jnp.max(masked, axis=-1), own_score)
    expo = jnp.where(valid, jnp.exp(masked - top[..., None]), 0.0)
    own_expo = jnp.exp(own_score - top)
    total = jnp.sum(expo, axis=-1) + own_expo
    weights = (expo / total[..., None]).astype(jnp.bfloat16)
    own_weight = (own_expo / total).astype(jnp.bfloat16)
    context = jnp.einsum(
        "rhc,rcv->rhv", weights, keys[:, :, :VDIM], preferred_element_type=jnp.float32
    )
    context = context + own_weight.astype(jnp.float32)[..., None] * newest[:, None, :VDIM].astype(
        jnp.float32
    )
    return context.astype(jnp.bfloat16)


def swap(block, q, j):
    dp_count, tp_count = lax.axis_size("dp"), lax.axis_size("tp")
    pairs = [
        (p * tp_count + t, (p ^ q) * tp_count + (t ^ j))
        for p in range(dp_count)
        for t in range(tp_count)
    ]
    return lax.ppermute(block, AXES, pairs)


def far_masks():
    masks = list(range(4, lax.axis_size("tp"), 4))
    return masks[1:] + masks[:1]


def quad():
    return [(q, y) for q in range(lax.axis_size("dp")) for y in (0, 2) if (q, y) != (0, 0)]


def gather_far(rows):
    return jnp.stack([rows] + [swap(rows, 0, j) for j in far_masks()], axis=0)


def feature_part(rows, part, count):
    size = rows.shape[-1] // count
    return lax.dynamic_slice_in_dim(rows, part * size, size, axis=rows.ndim - 1)


def near_parts(far, dp_rank, dp_count):
    far = far.reshape(-1, far.shape[-1])
    parts = [feature_part(far, dp_rank, dp_count)]
    for q, y in quad():
        parts.append(swap(feature_part(far, dp_rank ^ q, dp_count), q, y))
    return jnp.concatenate(parts, axis=0)


def gather_quad(far):
    far = far.reshape(-1, far.shape[-1])
    return [far] + [swap(far, q, y) for q, y in quad()]


def wide(block):
    return block.astype(jnp.float32)


def sum_dp(parts, dp_count):
    total, away = parts
    size = total.shape[0]
    for q in range(1, dp_count):
        total = total + wide(swap(away[(q - 1) * size : q * size], q, 0))
    return total


def reduce_core(mine, away, blocks):
    got = swap(away, 0, 1)
    size = mine.shape[0] // blocks
    return [wide(mine[at : at + size]) + wide(got[at : at + size]) for at in range(0, mine.shape[0], size)]


def reduce_far(blocks):
    out = blocks[0]
    for block, j in zip(blocks[1:], far_masks()):
        out = out + wide(swap(block.astype(jnp.bfloat16), 0, j))
    return out


def reduce_parts(near, dp_rank, dp_count, rows_dev):
    size = near[0].shape[1]
    parts = []
    for q in range(dp_count):
        part = near[2 * q] if q == 0 else wide(swap(near[2 * q].astype(jnp.bfloat16), q, 0))
        parts.append(part + wide(swap(near[2 * q + 1].astype(jnp.bfloat16), q, 2)))
    if dp_count == 2:
        first = dp_rank == 0
        full = jnp.concatenate([jnp.where(first, parts[0], parts[1]), jnp.where(first, parts[1], parts[0])], axis=1)
    else:
        full = jnp.zeros((parts[0].shape[0], size * dp_count), jnp.float32)
        for q in range(dp_count):
            full = lax.dynamic_update_slice_in_dim(full, parts[q], (dp_rank ^ q) * size, axis=1)
    return reduce_far([full[at : at + rows_dev] for at in range(0, full.shape[0], rows_dev)])


def reduce_rows(near, rows_dev):
    out = near[0]
    for q, y in quad():
        out = out + wide(swap(near[2 * q + y // 2].astype(jnp.bfloat16), q, y))
    return reduce_far([out[at : at + rows_dev] for at in range(0, out.shape[0], rows_dev)])


def cut_pieces(leaving):
    tp_count = lax.axis_size("tp")
    moving, layers, cache, lat = leaving.shape
    piece = layers * lat // tp_count
    turned = leaving.transpose(0, 1, 3, 2).reshape(moving, tp_count, piece, cache)
    return turned.transpose(1, 0, 2, 3)


def arrival_sources(group_dest):
    packets = group_dest.size
    moving = group_dest.shape[1]
    dest = group_dest.reshape(-1)
    at = jnp.arange(packets)
    earlier = (dest[:, None] == dest[None, :]) & (at[None, :] // moving < at[:, None] // moving)
    place = dest * moving + jnp.sum(earlier.astype(jnp.int32), axis=1)
    return jnp.sum(jnp.where(place[None, :] == at[:, None], at[None, :], 0), axis=1)


def sort_pieces(spread, source):
    packets = jnp.take(spread.reshape((-1,) + spread.shape[2:]), source, axis=0, mode="clip")
    return packets.reshape(spread.shape)


def join_pieces(home, shape):
    moving, layers, cache, lat = shape
    turned = home.transpose(1, 0, 2, 3).reshape(moving, layers, lat, cache)
    return turned.transpose(0, 1, 3, 2)


def in_hbm(weights):
    return pltpu.with_memory_space_constraint(weights, HBM)


def ring(copies, slots):
    count, make = copies
    for at in range(min(slots, count)):
        make(at).start()

    def free(at):
        @pl.when(at + slots < count)
        def _():
            make(at + slots).start()

    return (lambda at: make(at).wait()), free


def dense_kernel(groups, near_ref, other_ref, hbm, own_ref, away_ref, rows_ref, buf, sem):
    size = near_ref.shape[0] // groups
    steps = near_ref.shape[1] // DENSE_STEP

    def make(at):
        slot = lax.rem(at, SLOTS)
        return pltpu.make_async_copy(
            hbm.at[pl.ds(at * DENSE_STEP, DENSE_STEP)], buf.at[slot], sem.at[slot]
        )

    wait, free = ring((steps, make), SLOTS)
    for at in range(groups):
        part = slice(at * size, (at + 1) * size)
        rows_ref[2 * at * size : (2 * at + 1) * size] = near_ref[part]
        rows_ref[(2 * at + 1) * size : (2 * at + 2) * size] = other_ref[part]
    acc = jnp.zeros((rows_ref.shape[0], own_ref.shape[1]), jnp.float32)
    for at in range(steps):
        wait(at)
        rows = rows_ref[:, at * DENSE_STEP : (at + 1) * DENSE_STEP]
        acc = acc + jnp.dot(rows, buf[at % SLOTS], preferred_element_type=jnp.float32)
        free(at)
    own = own_ref.shape[0]
    own_ref[...] = acc[:own]
    away_ref[...] = acc[own:].astype(jnp.bfloat16)


def run_dense(near, other, weights, groups):
    count, width = 2 * near.shape[0], weights.shape[1]
    vmem, far = pl.BlockSpec(memory_space=pltpu.VMEM), pl.BlockSpec(memory_space=HBM)
    own = count // groups
    return pl.pallas_call(
        functools.partial(dense_kernel, groups),
        out_shape=(
            jax.ShapeDtypeStruct((own, width), jnp.float32),
            jax.ShapeDtypeStruct((count - own, width), jnp.bfloat16),
        ),
        in_specs=[vmem, vmem, far],
        out_specs=(vmem, vmem),
        scratch_shapes=[
            pltpu.VMEM((count, near.shape[1]), jnp.bfloat16),
            pltpu.VMEM((SLOTS, DENSE_STEP, width), jnp.bfloat16),
            pltpu.SemaphoreType.DMA((SLOTS,)),
        ],
        compiler_params=pltpu.CompilerParams(vmem_limit_bytes=DENSE_VMEM * 1024 * 1024),
    )(near, other, in_hbm(weights))


def expert_kernel(outs, experts, *refs):
    parts, refs = refs[:2], refs[2:]
    gate_hbm, up_hbm, down_hbm = refs[:3]
    results, refs = refs[3 : 3 + 2 * outs], refs[3 + 2 * outs :]
    rows_ref, tail_ref, inner_ref, gate_buf, up_buf, down_buf, gate_acc, up_acc, row_sem, gate_sem, up_sem, down_sem = refs
    half, width = rows_ref.shape[0] // 2, rows_ref.shape[1]
    span = width // outs

    def copies(hbm, buf, sem):
        def make(at):
            slot = lax.rem(at, SLOTS)
            return pltpu.make_async_copy(
                hbm.at[0, pl.ds(at * STEP, STEP)], buf.at[slot], sem.at[slot]
            )

        return width // STEP, make

    def make_down(at):
        slot = lax.rem(at, SLOTS)
        where = pl.ds(pl.multiple_of(at * DOWN_STEP, 128), DOWN_STEP)
        return pltpu.make_async_copy(down_hbm.at[0, :, where], down_buf.at[slot], down_sem.at[slot])

    moves = []
    for side in range(2):
        where = pl.ds(side * half, half)
        moves.append((parts[side].at[:, pl.ds(0, width)], rows_ref.at[where]))
        moves.append((parts[side].at[:, pl.ds(width, 128)], tail_ref.at[where]))
    moves = [pltpu.make_async_copy(*move, row_sem.at[at]) for at, move in enumerate(moves)]
    for move in moves:
        move.start()
    gate_wait, gate_free = ring(copies(gate_hbm, gate_buf, gate_sem), SLOTS)
    up_wait, up_free = ring(copies(up_hbm, up_buf, up_sem), SLOTS)
    down_wait, down_free = ring((width // DOWN_STEP, make_down), SLOTS)
    gate_acc[...] = jnp.zeros_like(gate_acc)
    up_acc[...] = jnp.zeros_like(up_acc)
    for move in moves:
        move.wait()

    @pl.loop(0, width // STEP)
    def _(at):
        rows = rows_ref[:, pl.ds(pl.multiple_of(at * STEP, 128), STEP)]
        slot = lax.rem(at, SLOTS)
        gate_wait(at)
        gate_acc[...] += jnp.dot(rows, gate_buf[slot], preferred_element_type=jnp.float32)
        gate_free(at)
        up_wait(at)
        up_acc[...] += jnp.dot(rows, up_buf[slot], preferred_element_type=jnp.float32)
        up_free(at)

    lane = lax.broadcasted_iota(jnp.int32, (1, 128), 1)
    rank = lax.axis_index("tp")
    mine = (lane == rank) | (lane == rank + experts)
    share = jnp.sum(jnp.where(mine, tail_ref[...].astype(jnp.float32), 0.0), axis=1, keepdims=True)
    gate = gate_acc[...]
    inner_ref[...] = (gate / (1.0 + jnp.exp(-gate)) * up_acc[...] * share).astype(jnp.bfloat16)

    for one in range(outs):
        near_ref, away_ref = results[2 * one : 2 * one + 2]
        first = one * (span // DOWN_STEP)

        @pl.loop(0, span // DOWN_STEP)
        def _(step, near_ref=near_ref, away_ref=away_ref, first=first):
            at = first + step
            down_wait(at)
            where = pl.ds(pl.multiple_of(step * DOWN_STEP, 128), DOWN_STEP)
            weights = down_buf[lax.rem(at, SLOTS)]
            out = jnp.dot(inner_ref[...], weights, preferred_element_type=jnp.float32)
            near_ref[:, where] = out[:half].astype(jnp.bfloat16)
            away_ref[:, where] = out[half:].astype(jnp.bfloat16)
            down_free(at)


def run_expert(near, other, gate_w, up_w, down_w, experts):
    count, width, hidden = 2 * near.shape[0], gate_w.shape[1], gate_w.shape[2]
    vmem, far = pl.BlockSpec(memory_space=pltpu.VMEM), pl.BlockSpec(memory_space=HBM)
    total = pltpu.VMEM((count, hidden), jnp.float32)
    weights = pltpu.VMEM((SLOTS, STEP, hidden), jnp.bfloat16)
    half = jax.ShapeDtypeStruct((count // 2, width // DOWN_CUTS), jnp.bfloat16)
    sems = pltpu.SemaphoreType.DMA((SLOTS,))
    out = pl.pallas_call(
        functools.partial(expert_kernel, DOWN_CUTS, experts),
        out_shape=(half,) * (2 * DOWN_CUTS),
        in_specs=[pl.BlockSpec(memory_space=pl.ANY)] * 2 + [far] * 3,
        out_specs=(vmem,) * (2 * DOWN_CUTS),
        scratch_shapes=[
            pltpu.VMEM((count, width), jnp.bfloat16),
            pltpu.VMEM((count, 128), jnp.bfloat16),
            pltpu.VMEM((count, hidden), jnp.bfloat16),
            weights,
            weights,
            pltpu.VMEM((SLOTS, hidden, DOWN_STEP), jnp.bfloat16),
            total,
            total,
            pltpu.SemaphoreType.DMA((4,)),
            sems,
            sems,
            sems,
        ],
        compiler_params=pltpu.CompilerParams(vmem_limit_bytes=32 * 1024 * 1024),
    )(near, other, in_hbm(gate_w), in_hbm(up_w), in_hbm(down_w))
    return [out[2 * at : 2 * at + 2] for at in range(DOWN_CUTS)]


def on_device(
    queries,
    new_latent,
    resident,
    leaving,
    res_len,
    leave_len,
    mig_dest,
    stream,
    dense_gain,
    w_gate,
    w_up,
    w_down,
    moe_gain,
    expert_gate,
    expert_up,
    expert_down,
    expert_ids,
    gate_scores,
):
    tp_count = lax.axis_size("tp")
    dp_count = lax.axis_size("dp")
    tp_rank = lax.axis_index("tp")
    dp_rank = lax.axis_index("dp")
    group_dest = lax.dynamic_slice_in_dim(mig_dest, dp_rank * tp_count, tp_count, 0)
    group_len = lax.dynamic_slice_in_dim(leave_len, dp_rank * tp_count, tp_count, 0)
    rows_dev = stream.shape[0]
    normed = rms_scale(stream, dense_gain)
    near = near_parts(gather_far(normed), dp_rank, dp_count)
    other = swap(near, 0, 1)
    near, outgoing = lax.optimization_barrier((near, cut_pieces(leaving)))
    gate_parts = run_dense(near, other, w_gate, dp_count)
    spread = lax.all_to_all(outgoing, "tp", split_axis=0, concat_axis=0, tiled=True)
    gate = sum_dp(gate_parts, dp_count)
    up = sum_dp(run_dense(near, other, w_up, dp_count), dp_count)
    hidden = (jax.nn.silu(gate) * up).astype(jnp.bfloat16)
    near = []
    for q in range(dp_count):
        block = swap(hidden, q, 0) if q else hidden
        down = jnp.dot(block, w_down, preferred_element_type=jnp.float32).astype(jnp.bfloat16)
        half = down.shape[0] // 2
        near += reduce_core(down[:half], down[half:], 2)
    stay = resident.shape[0]
    context_stay = attend(queries[:stay], resident, res_len, new_latent[:stay])
    near[-1], context_stay = lax.optimization_barrier((near[-1], context_stay))
    near[0], spread = lax.optimization_barrier((near[0], spread))
    ffn = reduce_parts(near, dp_rank, dp_count, rows_dev)
    middle = (stream.astype(jnp.float32) + ffn).astype(jnp.bfloat16)
    mixed = rms_scale(middle, moe_gain)

    shares = gate_scores / jnp.sum(gate_scores, axis=1, keepdims=True) * ROUTE_SCALE
    experts = tp_count * expert_gate.shape[0]
    chosen = expert_ids[:, :, None] == jnp.arange(experts)[None, None, :]
    table = jnp.sum(jnp.where(chosen, shares[:, :, None], 0.0), axis=1)
    high = table.astype(jnp.bfloat16)
    low = (table - wide(high)).astype(jnp.bfloat16)
    tail = jnp.pad(jnp.concatenate([high, low], axis=1), ((0, 0), (0, 128 - 2 * experts)))
    width = mixed.shape[1] // CUTS
    pieces = [mixed[:, at * width : (at + 1) * width] for at in range(CUTS)]
    pieces[-1] = jnp.concatenate([pieces[-1], tail], axis=1)
    homing = sort_pieces(spread, arrival_sources(group_dest))
    cuts = [gather_quad(gather_far(piece)) for piece in pieces]
    cuts[0][-1], homing = lax.optimization_barrier((cuts[0][-1], homing))
    near = [lax.optimization_barrier(jnp.concatenate(row, axis=1)) for row in zip(*cuts)]
    near = jnp.concatenate(near, axis=0)
    halves = run_expert(near, swap(near, 0, 1), expert_gate, expert_up, expert_down, experts)
    out = []
    width = mixed.shape[1] // DOWN_CUTS
    sums = [reduce_core(*half, 2 * dp_count) for half in halves]
    home = lax.all_to_all(homing, "tp", split_axis=0, concat_axis=0, tiled=True)
    arrived = join_pieces(home, leaving.shape)
    for at in range(DOWN_CUTS):
        routed = reduce_rows(sums[at], rows_dev)
        out.append(wide(middle[:, at * width : (at + 1) * width]) + routed)
    moving = leaving.shape[0]
    source = arrival_sources(group_dest)
    mine = lax.dynamic_slice_in_dim(source, tp_rank * moving, moving, 0)
    arrived_len = jnp.take(group_len.reshape(-1), mine, axis=0, mode="clip")
    context_moved = attend(queries[stay:], arrived[:, 0], arrived_len, new_latent[stay:])
    context = jnp.concatenate([context_stay, context_moved], axis=0)

    stream_out = jnp.concatenate(out, axis=1).astype(jnp.bfloat16)
    return (context, arrived, stream_out)


def solution(mesh):
    placed = (
        P(("dp", "tp"), None, None),
        P(("dp", "tp"), None),
        P(("dp", "tp"), None, None),
        P(("dp", "tp"), None, None, None),
        P(("dp", "tp")),
        P(),
        P(),
        P(("dp", "tp"), None),
        P(),
        P("dp", "tp"),
        P("dp", "tp"),
        P("tp", "dp"),
        P(),
        P("tp", None, "dp"),
        P("tp", None, "dp"),
        P("tp", "dp", None),
        P(("dp", "tp"), None),
        P(("dp", "tp"), None),
    )
    return jax.shard_map(
        on_device,
        mesh=mesh,
        in_specs=placed,
        out_specs=(
            P(("dp", "tp"), None, None),
            P(("dp", "tp"), None, None, None),
            P(("dp", "tp"), None),
        ),
        check_vma=False,
    )
```

```python
import functools

import jax
import jax.numpy as jnp
from jax import lax
from jax.experimental import pallas as pl
from jax.experimental.pallas import tpu as pltpu
from jax.sharding import PartitionSpec as P

VDIM = 512
QKD = 192


EPS = 1e-06
ROUTE_SCALE = 2.5
AXES = ("dp", "tp")
CUTS = 2
DOWN_CUTS = 2
DOWN_STEP = 896
STEP = 1024
SLOTS = 3
DENSE_STEPS = (512, 896)
DENSE_VMEM = 14
HBM = pltpu.MemorySpace.HBM


def rms_scale(rows, gain):
    values = rows.astype(jnp.float32)
    mean_square = jnp.mean(values * values, axis=-1, keepdims=True)
    return (values * lax.rsqrt(mean_square + EPS) * gain).astype(jnp.bfloat16)


def attend(queries, keys, lengths, newest):
    scale = QKD ** (-0.5)
    scores = jnp.einsum("rhl,rcl->rhc", queries, keys, preferred_element_type=jnp.float32) * scale
    positions = jnp.arange(keys.shape[1])
    valid = positions[None, None, :] < lengths[:, None, None]
    masked = jnp.where(valid, scores, -1e30)
    own_score = (
        jnp.einsum("rhl,rl->rh", queries, newest, preferred_element_type=jnp.float32) * scale
    )
    top = jnp.maximum(jnp.max(masked, axis=-1), own_score)
    expo = jnp.where(valid, jnp.exp(masked - top[..., None]), 0.0)
    own_expo = jnp.exp(own_score - top)
    total = jnp.sum(expo, axis=-1) + own_expo
    weights = (expo / total[..., None]).astype(jnp.bfloat16)
    own_weight = (own_expo / total).astype(jnp.bfloat16)
    context = jnp.einsum(
        "rhc,rcv->rhv", weights, keys[:, :, :VDIM], preferred_element_type=jnp.float32
    )
    context = context + own_weight.astype(jnp.float32)[..., None] * newest[:, None, :VDIM].astype(
        jnp.float32
    )
    return context.astype(jnp.bfloat16)


def swap(block, q, j):
    dp_count, tp_count = lax.axis_size("dp"), lax.axis_size("tp")
    pairs = [
        (p * tp_count + t, (p ^ q) * tp_count + (t ^ j))
        for p in range(dp_count)
        for t in range(tp_count)
    ]
    return lax.ppermute(block, AXES, pairs)


def far_masks():
    masks = list(range(4, lax.axis_size("tp"), 4))
    return masks[1:] + masks[:1]


def quad():
    return [(q, y) for q in range(lax.axis_size("dp")) for y in (0, 2) if (q, y) != (0, 0)]


def gather_far(rows):
    return jnp.stack([rows] + [swap(rows, 0, j) for j in far_masks()], axis=0)


def feature_part(rows, part, count):
    size = rows.shape[-1] // count
    return lax.dynamic_slice_in_dim(rows, part * size, size, axis=rows.ndim - 1)


def near_parts(far, dp_rank, dp_count):
    far = far.reshape(-1, far.shape[-1])
    parts = [feature_part(far, dp_rank, dp_count)]
    for q, y in quad():
        parts.append(swap(feature_part(far, dp_rank ^ q, dp_count), q, y))
    return jnp.concatenate(parts, axis=0)


def gather_quad(far):
    far = far.reshape(-1, far.shape[-1])
    return [far] + [swap(far, q, y) for q, y in quad()]


def wide(block):
    return block.astype(jnp.float32)


def sum_dp(parts, dp_count):
    total, away = parts
    size = total.shape[0]
    for q in range(1, dp_count):
        total = total + wide(swap(away[(q - 1) * size : q * size], q, 0))
    return total


def reduce_core(mine, away, blocks):
    got = swap(away, 0, 1)
    size = mine.shape[0] // blocks
    return [wide(mine[at : at + size]) + wide(got[at : at + size]) for at in range(0, mine.shape[0], size)]


def reduce_far(blocks):
    out = blocks[0]
    for block, j in zip(blocks[1:], far_masks()):
        out = out + wide(swap(block.astype(jnp.bfloat16), 0, j))
    return out


def reduce_parts(near, dp_rank, dp_count, rows_dev):
    size = near[0].shape[1]
    parts = []
    for q in range(dp_count):
        part = near[2 * q] if q == 0 else wide(swap(near[2 * q].astype(jnp.bfloat16), q, 0))
        parts.append(part + wide(swap(near[2 * q + 1].astype(jnp.bfloat16), q, 2)))
    if dp_count == 2:
        first = dp_rank == 0
        full = jnp.concatenate([jnp.where(first, parts[0], parts[1]), jnp.where(first, parts[1], parts[0])], axis=1)
    else:
        full = jnp.zeros((parts[0].shape[0], size * dp_count), jnp.float32)
        for q in range(dp_count):
            full = lax.dynamic_update_slice_in_dim(full, parts[q], (dp_rank ^ q) * size, axis=1)
    return reduce_far([full[at : at + rows_dev] for at in range(0, full.shape[0], rows_dev)])


def reduce_rows(near, rows_dev):
    out = near[0]
    for q, y in quad():
        out = out + wide(swap(near[2 * q + y // 2].astype(jnp.bfloat16), q, y))
    return reduce_far([out[at : at + rows_dev] for at in range(0, out.shape[0], rows_dev)])


def cut_pieces(leaving):
    tp_count = lax.axis_size("tp")
    moving, layers, cache, lat = leaving.shape
    piece = layers * lat // tp_count
    turned = leaving.transpose(0, 1, 3, 2).reshape(moving, tp_count, piece, cache)
    return turned.transpose(1, 0, 2, 3)


def arrival_sources(group_dest):
    packets = group_dest.size
    moving = group_dest.shape[1]
    dest = group_dest.reshape(-1)
    at = jnp.arange(packets)
    earlier = (dest[:, None] == dest[None, :]) & (at[None, :] // moving < at[:, None] // moving)
    place = dest * moving + jnp.sum(earlier.astype(jnp.int32), axis=1)
    return jnp.sum(jnp.where(place[None, :] == at[:, None], at[None, :], 0), axis=1)


def sort_pieces(spread, source):
    packets = jnp.take(spread.reshape((-1,) + spread.shape[2:]), source, axis=0, mode="clip")
    return packets.reshape(spread.shape)


def join_pieces(home, shape):
    moving, layers, cache, lat = shape
    turned = home.transpose(1, 0, 2, 3).reshape(moving, layers, lat, cache)
    return turned.transpose(0, 1, 3, 2)


def in_hbm(weights):
    return pltpu.with_memory_space_constraint(weights, HBM)


def ring(copies, slots):
    count, make = copies
    for at in range(min(slots, count)):
        make(at).start()

    def free(at):
        @pl.when(at + slots < count)
        def _():
            make(at + slots).start()

    return (lambda at: make(at).wait()), free


def dense_kernel(groups, near_ref, other_ref, hbm, own_ref, away_ref, rows_ref, buf, sem):
    size = near_ref.shape[0] // groups
    piece = buf.shape[1]
    steps = near_ref.shape[1] // piece

    def make(at):
        slot = lax.rem(at, SLOTS)
        return pltpu.make_async_copy(
            hbm.at[pl.ds(at * piece, piece)], buf.at[slot], sem.at[slot]
        )

    wait, free = ring((steps, make), SLOTS)
    for at in range(groups):
        part = slice(at * size, (at + 1) * size)
        rows_ref[2 * at * size : (2 * at + 1) * size] = near_ref[part]
        rows_ref[(2 * at + 1) * size : (2 * at + 2) * size] = other_ref[part]
    acc = jnp.zeros((rows_ref.shape[0], own_ref.shape[1]), jnp.float32)
    for at in range(steps):
        wait(at)
        rows = rows_ref[:, at * piece : (at + 1) * piece]
        acc = acc + jnp.dot(rows, buf[at % SLOTS], preferred_element_type=jnp.float32)
        free(at)
    own = own_ref.shape[0]
    own_ref[...] = acc[:own]
    away_ref[...] = acc[own:].astype(jnp.bfloat16)


def run_dense(near, other, weights, groups):
    count, width = 2 * near.shape[0], weights.shape[1]
    vmem, far = pl.BlockSpec(memory_space=pltpu.VMEM), pl.BlockSpec(memory_space=HBM)
    own = count // groups
    step = next(step for step in DENSE_STEPS if near.shape[1] % step == 0)
    return pl.pallas_call(
        functools.partial(dense_kernel, groups),
        out_shape=(
            jax.ShapeDtypeStruct((own, width), jnp.float32),
            jax.ShapeDtypeStruct((count - own, width), jnp.bfloat16),
        ),
        in_specs=[vmem, vmem, far],
        out_specs=(vmem, vmem),
        scratch_shapes=[
            pltpu.VMEM((count, near.shape[1]), jnp.bfloat16),
            pltpu.VMEM((SLOTS, step, width), jnp.bfloat16),
            pltpu.SemaphoreType.DMA((SLOTS,)),
        ],
        compiler_params=pltpu.CompilerParams(vmem_limit_bytes=DENSE_VMEM * 1024 * 1024),
    )(near, other, in_hbm(weights))


def expert_kernel(outs, experts, *refs):
    parts, refs = refs[:2], refs[2:]
    gate_hbm, up_hbm, down_hbm = refs[:3]
    results, refs = refs[3 : 3 + 2 * outs], refs[3 + 2 * outs :]
    rows_ref, tail_ref, inner_ref, gate_buf, up_buf, down_buf, gate_acc, up_acc, row_sem, gate_sem, up_sem, down_sem = refs
    half, width = rows_ref.shape[0] // 2, rows_ref.shape[1]
    span = width // outs

    def copies(hbm, buf, sem):
        def make(at):
            slot = lax.rem(at, SLOTS)
            return pltpu.make_async_copy(
                hbm.at[0, pl.ds(at * STEP, STEP)], buf.at[slot], sem.at[slot]
            )

        return width // STEP, make

    def make_down(at):
        slot = lax.rem(at, SLOTS)
        where = pl.ds(pl.multiple_of(at * DOWN_STEP, 128), DOWN_STEP)
        return pltpu.make_async_copy(down_hbm.at[0, :, where], down_buf.at[slot], down_sem.at[slot])

    moves = []
    for side in range(2):
        where = pl.ds(side * half, half)
        moves.append((parts[side].at[:, pl.ds(0, width)], rows_ref.at[where]))
        moves.append((parts[side].at[:, pl.ds(width, 128)], tail_ref.at[where]))
    moves = [pltpu.make_async_copy(*move, row_sem.at[at]) for at, move in enumerate(moves)]
    for move in moves:
        move.start()
    gate_wait, gate_free = ring(copies(gate_hbm, gate_buf, gate_sem), SLOTS)
    up_wait, up_free = ring(copies(up_hbm, up_buf, up_sem), SLOTS)
    down_wait, down_free = ring((width // DOWN_STEP, make_down), SLOTS)
    gate_acc[...] = jnp.zeros_like(gate_acc)
    up_acc[...] = jnp.zeros_like(up_acc)
    for move in moves:
        move.wait()

    @pl.loop(0, width // STEP)
    def _(at):
        rows = rows_ref[:, pl.ds(pl.multiple_of(at * STEP, 128), STEP)]
        slot = lax.rem(at, SLOTS)
        gate_wait(at)
        gate_acc[...] += jnp.dot(rows, gate_buf[slot], preferred_element_type=jnp.float32)
        gate_free(at)
        up_wait(at)
        up_acc[...] += jnp.dot(rows, up_buf[slot], preferred_element_type=jnp.float32)
        up_free(at)

    lane = lax.broadcasted_iota(jnp.int32, (1, 128), 1)
    rank = lax.axis_index("tp")
    mine = (lane == rank) | (lane == rank + experts)
    share = jnp.sum(jnp.where(mine, tail_ref[...].astype(jnp.float32), 0.0), axis=1, keepdims=True)
    gate = gate_acc[...]
    inner_ref[...] = (gate / (1.0 + jnp.exp(-gate)) * up_acc[...] * share).astype(jnp.bfloat16)

    for one in range(outs):
        near_ref, away_ref = results[2 * one : 2 * one + 2]
        first = one * (span // DOWN_STEP)

        @pl.loop(0, span // DOWN_STEP)
        def _(step, near_ref=near_ref, away_ref=away_ref, first=first):
            at = first + step
            down_wait(at)
            where = pl.ds(pl.multiple_of(step * DOWN_STEP, 128), DOWN_STEP)
            weights = down_buf[lax.rem(at, SLOTS)]
            out = jnp.dot(inner_ref[...], weights, preferred_element_type=jnp.float32)
            near_ref[:, where] = out[:half].astype(jnp.bfloat16)
            away_ref[:, where] = out[half:].astype(jnp.bfloat16)
            down_free(at)


def run_expert(near, other, gate_w, up_w, down_w, experts):
    count, width, hidden = 2 * near.shape[0], gate_w.shape[1], gate_w.shape[2]
    vmem, far = pl.BlockSpec(memory_space=pltpu.VMEM), pl.BlockSpec(memory_space=HBM)
    total = pltpu.VMEM((count, hidden), jnp.float32)
    weights = pltpu.VMEM((SLOTS, STEP, hidden), jnp.bfloat16)
    half = jax.ShapeDtypeStruct((count // 2, width // DOWN_CUTS), jnp.bfloat16)
    sems = pltpu.SemaphoreType.DMA((SLOTS,))
    out = pl.pallas_call(
        functools.partial(expert_kernel, DOWN_CUTS, experts),
        out_shape=(half,) * (2 * DOWN_CUTS),
        in_specs=[pl.BlockSpec(memory_space=pl.ANY)] * 2 + [far] * 3,
        out_specs=(vmem,) * (2 * DOWN_CUTS),
        scratch_shapes=[
            pltpu.VMEM((count, width), jnp.bfloat16),
            pltpu.VMEM((count, 128), jnp.bfloat16),
            pltpu.VMEM((count, hidden), jnp.bfloat16),
            weights,
            weights,
            pltpu.VMEM((SLOTS, hidden, DOWN_STEP), jnp.bfloat16),
            total,
            total,
            pltpu.SemaphoreType.DMA((4,)),
            sems,
            sems,
            sems,
        ],
        compiler_params=pltpu.CompilerParams(vmem_limit_bytes=32 * 1024 * 1024),
    )(near, other, in_hbm(gate_w), in_hbm(up_w), in_hbm(down_w))
    return [out[2 * at : 2 * at + 2] for at in range(DOWN_CUTS)]


def on_device(
    queries,
    new_latent,
    resident,
    leaving,
    res_len,
    leave_len,
    mig_dest,
    stream,
    dense_gain,
    w_gate,
    w_up,
    w_down,
    moe_gain,
    expert_gate,
    expert_up,
    expert_down,
    expert_ids,
    gate_scores,
):
    tp_count = lax.axis_size("tp")
    dp_count = lax.axis_size("dp")
    tp_rank = lax.axis_index("tp")
    dp_rank = lax.axis_index("dp")
    group_dest = lax.dynamic_slice_in_dim(mig_dest, dp_rank * tp_count, tp_count, 0)
    group_len = lax.dynamic_slice_in_dim(leave_len, dp_rank * tp_count, tp_count, 0)
    rows_dev = stream.shape[0]
    normed = rms_scale(stream, dense_gain)
    near = near_parts(gather_far(normed), dp_rank, dp_count)
    other = swap(near, 0, 1)
    near, outgoing = lax.optimization_barrier((near, cut_pieces(leaving)))
    gate_parts = run_dense(near, other, w_gate, dp_count)
    spread = lax.all_to_all(outgoing, "tp", split_axis=0, concat_axis=0, tiled=True)
    gate = sum_dp(gate_parts, dp_count)
    up = sum_dp(run_dense(near, other, w_up, dp_count), dp_count)
    hidden = (jax.nn.silu(gate) * up).astype(jnp.bfloat16)
    near = []
    for q in range(dp_count):
        block = swap(hidden, q, 0) if q else hidden
        down = jnp.dot(block, w_down, preferred_element_type=jnp.float32).astype(jnp.bfloat16)
        half = down.shape[0] // 2
        near += reduce_core(down[:half], down[half:], 2)
    stay = resident.shape[0]
    context_stay = attend(queries[:stay], resident, res_len, new_latent[:stay])
    near[-1], context_stay = lax.optimization_barrier((near[-1], context_stay))
    near[0], spread = lax.optimization_barrier((near[0], spread))
    ffn = reduce_parts(near, dp_rank, dp_count, rows_dev)
    middle = (stream.astype(jnp.float32) + ffn).astype(jnp.bfloat16)
    mixed = rms_scale(middle, moe_gain)

    shares = gate_scores / jnp.sum(gate_scores, axis=1, keepdims=True) * ROUTE_SCALE
    experts = tp_count * expert_gate.shape[0]
    chosen = expert_ids[:, :, None] == jnp.arange(experts)[None, None, :]
    table = jnp.sum(jnp.where(chosen, shares[:, :, None], 0.0), axis=1)
    high = table.astype(jnp.bfloat16)
    low = (table - wide(high)).astype(jnp.bfloat16)
    tail = jnp.pad(jnp.concatenate([high, low], axis=1), ((0, 0), (0, 128 - 2 * experts)))
    width = mixed.shape[1] // CUTS
    pieces = [mixed[:, at * width : (at + 1) * width] for at in range(CUTS)]
    pieces[-1] = jnp.concatenate([pieces[-1], tail], axis=1)
    homing = sort_pieces(spread, arrival_sources(group_dest))
    cuts = [gather_quad(gather_far(piece)) for piece in pieces]
    cuts[0][-1], homing = lax.optimization_barrier((cuts[0][-1], homing))
    near = [lax.optimization_barrier(jnp.concatenate(row, axis=1)) for row in zip(*cuts)]
    near = jnp.concatenate(near, axis=0)
    halves = run_expert(near, swap(near, 0, 1), expert_gate, expert_up, expert_down, experts)
    out = []
    width = mixed.shape[1] // DOWN_CUTS
    sums = [reduce_core(*half, 2 * dp_count) for half in halves]
    home = lax.all_to_all(homing, "tp", split_axis=0, concat_axis=0, tiled=True)
    arrived = join_pieces(home, leaving.shape)
    for at in range(DOWN_CUTS):
        routed = reduce_rows(sums[at], rows_dev)
        out.append(wide(middle[:, at * width : (at + 1) * width]) + routed)
    moving = leaving.shape[0]
    source = arrival_sources(group_dest)
    mine = lax.dynamic_slice_in_dim(source, tp_rank * moving, moving, 0)
    arrived_len = jnp.take(group_len.reshape(-1), mine, axis=0, mode="clip")
    context_moved = attend(queries[stay:], arrived[:, 0], arrived_len, new_latent[stay:])
    context = jnp.concatenate([context_stay, context_moved], axis=0)

    stream_out = jnp.concatenate(out, axis=1).astype(jnp.bfloat16)
    return (context, arrived, stream_out)


def solution(mesh):
    placed = (
        P(("dp", "tp"), None, None),
        P(("dp", "tp"), None),
        P(("dp", "tp"), None, None),
        P(("dp", "tp"), None, None, None),
        P(("dp", "tp")),
        P(),
        P(),
        P(("dp", "tp"), None),
        P(),
        P("dp", "tp"),
        P("dp", "tp"),
        P("tp", "dp"),
        P(),
        P("tp", None, "dp"),
        P("tp", None, "dp"),
        P("tp", "dp", None),
        P(("dp", "tp"), None),
        P(("dp", "tp"), None),
    )
    return jax.shard_map(
        on_device,
        mesh=mesh,
        in_specs=placed,
        out_specs=(
            P(("dp", "tp"), None, None),
            P(("dp", "tp"), None, None, None),
            P(("dp", "tp"), None),
        ),
        check_vma=False,
    )
```
